1024 devices in a mesh: dp: 128 (over y, z_lo, core), mp: 8 (over x, z_hi).
Axes of the slice: x: 4, y: 4, z: 32 (z_hi: 2, z_lo: 16; z = z_hi * 16 + z_lo), core: 2. Of those that a mesh axis runs over, the one named last changes fastest.
Arguments:
- queries: bfloat16 [128, 256, 3072], P('dp', None, 'mp'), may hold values from -6 to 6
- attn_keys: bfloat16 [128, 256, 3072], P('dp', None, 'mp'), may hold values from -6 to 6
- attn_values: bfloat16 [128, 256, 3072], P('dp', None, 'mp'), may hold values from -6 to 6
- out_weight: bfloat16 [3072, 3072], P('dp', 'mp'), may hold values from -0.109375 to 0.109375
- grad_out: bfloat16 [128, 256, 3072], P('dp', 'mp'), may hold values from -96 to 96
Outputs:
- grad_queries: bfloat16 [128, 256, 3072], P('dp', None, 'mp')
- grad_keys: bfloat16 [128, 256, 3072], P('dp', None, 'mp')
- grad_values: bfloat16 [128, 256, 3072], P('dp', None, 'mp')
The draws below stay inside these ranges and needn't reach their ends.
All inputs are finite; a program needn't handle non-finite values.
Results may differ from the reference program's by a relative error of at most 0.0095.
Values may be sent and summed in bfloat16 or wider, within the bound.
No kernel may reach another device: no remote copies, remote signals or barrier semaphores. Data moves between devices by JAX's collectives and lax.ppermute only.
A program may use at most 32 MiB of HBM per device.

```python
import math
import jax
import jax.numpy as jnp
from jax import lax

D = 3072
HD = 128
PATCHES = 256
HEADS = 24
BATCH = 128


def draw_queries(key, part):
    key = jax.random.fold_in(key, 1)
    array_shape = (BATCH, PATCHES, HEADS * HD)
    result = jnp.clip(jax.random.normal(key, array_shape, jnp.float32), -6.0, 6.0)
    return result.astype(jnp.bfloat16)


def draw_attn_keys(key, part):
    key = jax.random.fold_in(key, 2)
    array_shape = (BATCH, PATCHES, HEADS * HD)
    result = jnp.clip(jax.random.normal(key, array_shape, jnp.float32), -6.0, 6.0)
    return result.astype(jnp.bfloat16)


def strengthened(drawn, rng, source, target, parts, factor):
    def block_of(axis_at):
        return (jnp.arange(drawn.shape[axis_at]) // (drawn.shape[axis_at] // parts)).reshape((-1,) + (1,) * (drawn.ndim - 1 - axis_at))

    near = jax.random.permutation(rng, parts)[block_of(target)]
    second = (block_of(target) + parts // 2) % parts
    return jnp.where((block_of(source) == near) | (block_of(source) == second), factor * drawn, drawn)


def shard_levels(own_key, dims, split, smallest, largest):
    def one(axis_at, parts):
        heights = jax.random.uniform(jax.random.fold_in(jax.random.fold_in(own_key, 6), axis_at), (parts,), jnp.float32, smallest / len(split), largest / len(split))
        return jnp.repeat(jnp.exp(heights), dims[axis_at] // parts).reshape((-1,) + (1,) * (len(dims) - axis_at - 1))

    factor_of = one(*split[0])
    for cut in split[1:]:
        factor_of = factor_of * one(*cut)
    return factor_of


def bell_draw(key, extent, scale, most, split=(), dtype=jnp.bfloat16):
    loudness = shard_levels(key, extent, split, -0.22, 0.18) if split else 1.0
    entries = jax.random.normal(key, extent, jnp.float32) * scale * loudness
    return jnp.minimum(jnp.maximum(entries, -most), most).astype(dtype)


def heavy_noise(stream_key, shape, width, bound, shards, heavy, dtype=jnp.bfloat16):
    entries = width * jax.random.normal(stream_key, shape, jnp.float32)
    if shards:
        entries = entries * shard_levels(stream_key, shape, shards, -0.22, 0.18)
    return jnp.clip(strengthened(entries, jax.random.fold_in(stream_key, 3), *heavy), -bound, bound).astype(dtype)


def setup_inputs(seed: int = 0) -> dict:
    keys = jax.random.split(jax.random.key(seed), 6)
    return {
        "queries": draw_queries(jax.random.fold_in(keys[5], 71), 0),
        "attn_keys": draw_attn_keys(jax.random.fold_in(keys[5], 71), 0),
        "attn_values": bell_draw(keys[2], (BATCH, PATCHES, HEADS * HD), 1.0, 6.0, ((0, 128), (2, 8))),
        "out_weight": bell_draw(keys[3], (D, HEADS * HD), (HEADS * HD) ** -0.5, 0.109375, ((0, 128), (1, 8))),
        "grad_out": heavy_noise(keys[4], (BATCH, PATCHES, D), 4.0, 96.0, ((0, 128), (1, 8)), (0, 2, 128, 5.5)),
    }


def image_grads(query_rows, key_rows, value_rows, grad_rows, out_weight):
    patches = query_rows.shape[0]
    head_count = query_rows.shape[1] // HD
    score_scale = 1.0 / math.sqrt(HD)
    query_heads = query_rows.reshape(patches, head_count, HD).astype(jnp.float32)
    key_heads = key_rows.reshape(patches, head_count, HD).astype(jnp.float32)
    value_heads = value_rows.reshape(patches, head_count, HD).astype(jnp.float32)
    scores = jnp.einsum('ihe,jhe->hij', query_heads, key_heads) * score_scale
    shifted = scores - lax.optimization_barrier(jnp.max(scores, axis=-1, keepdims=True))
    raised = jnp.exp(shifted)
    attention = raised / lax.optimization_barrier(jnp.sum(raised, axis=-1, keepdims=True))
    rounded = lax.optimization_barrier(attention.astype(jnp.bfloat16)).astype(jnp.float32)
    grad_attn = jnp.dot(grad_rows, out_weight, preferred_element_type=jnp.float32).astype(jnp.bfloat16)
    grad_heads = lax.optimization_barrier(grad_attn).astype(jnp.float32).reshape(patches, head_count, HD)
    grad_vals = jnp.einsum('hij,ihe->jhe', rounded, grad_heads).astype(jnp.bfloat16)
    grad_probs = jnp.einsum('ihe,jhe->hij', grad_heads, value_heads)
    row_inner = lax.optimization_barrier(jnp.sum(attention * grad_probs, axis=-1, keepdims=True))
    grad_scores = (attention * (grad_probs - row_inner) * score_scale).astype(jnp.bfloat16)
    grad_scores = lax.optimization_barrier(grad_scores).astype(jnp.float32)
    grad_query = jnp.einsum('hij,jhe->ihe', grad_scores, key_heads).astype(jnp.bfloat16)
    grad_key = jnp.einsum('hij,ihe->jhe', grad_scores, query_heads).astype(jnp.bfloat16)
    width_all = head_count * HD
    return (grad_query.reshape(patches, width_all), grad_key.reshape(patches, width_all), grad_vals.reshape(patches, width_all))

def reference(queries, attn_keys, attn_values, out_weight, grad_out):

    def step_image(items):
        query_rows, key_rows, value_rows, grad_rows = items
        return image_grads(query_rows, key_rows, value_rows, grad_rows, out_weight)
    stacked = lax.map(step_image, (queries, attn_keys, attn_values, grad_out))
    return (stacked[0], stacked[1], stacked[2])
```

```python
import math

import jax
import jax.numpy as jnp
import numpy as np
from jax import lax
from jax.experimental import pallas as pl
from jax.experimental.pallas import tpu as pltpu
from jax.sharding import PartitionSpec as P

HD = 128
AXES = ("dp", "mp")
NY, NZ, NC, NX, NH = 4, 16, 2, 4, 2


def exchange(y=0, z=0, core=0, x=0, half=0):
    pairs = []
    for dp in range(NY * NZ * NC):
        other = dp ^ (y * NZ * NC + z * NC + core)
        for mp in range(NX * NH):
            pairs.append((dp * NX * NH + mp, other * NX * NH + (mp ^ (x * NH + half))))
    return pairs


def swap(value, **moves):
    return lax.ppermute(value, AXES, exchange(**moves))


def nt(a, b):
    return lax.dot_general(a, b, (((1,), (1,)), ((), ())), preferred_element_type=jnp.float32)


def tn(a, b):
    return lax.dot_general(a, b, (((0,), (0,)), ((), ())), preferred_element_type=jnp.float32)


def nn(a, b):
    return lax.dot_general(a, b, (((1,), (0,)), ((), ())), preferred_element_type=jnp.float32)


def attention_kernel(q_ref, k_ref, out_ref):
    scale = 1.0 / math.sqrt(HD)
    for head in range(q_ref.shape[1] // HD):
        cols = pl.ds(head * HD, HD)
        scores = nt(q_ref[:, cols], k_ref[:, cols]) * scale
        raised = jnp.exp(scores - jnp.max(scores, axis=-1, keepdims=True))
        out_ref[head] = raised / jnp.sum(raised, axis=-1, keepdims=True)


def tail_kernel(rows_ref, attn_ref, q_ref, k_ref, v_ref, *refs):
    n_g = NX * NH
    n_w = NY * NC
    g_refs, w_refs = refs[:n_g], refs[n_g:n_g + n_w]
    gq_ref, gk_ref, gv_ref, grad_ref = refs[n_g + n_w:]
    scale = 1.0 / math.sqrt(HD)
    part, depth = g_refs[0].shape[0], w_refs[0].shape[0]
    total = None
    for piece in range(n_w):
        cols = pl.ds(piece * depth, depth)
        left = jnp.concatenate([g[:, cols] for g in g_refs], axis=0)
        term = nn(left, w_refs[piece][...])
        total = term if total is None else total + term
    total = total.astype(jnp.bfloat16)
    for slot in range(n_g):
        row = pl.multiple_of(rows_ref[slot] * part, part)
        grad_ref[pl.ds(row, part), :] = total[slot * part:(slot + 1) * part]
    for head in range(q_ref.shape[1] // HD):
        cols = pl.ds(head * HD, HD)
        grad = grad_ref[:, cols]
        attn = attn_ref[head]
        gv_ref[:, cols] = tn(attn.astype(jnp.bfloat16), grad).astype(jnp.bfloat16)
        probs = nt(grad, v_ref[:, cols])
        inner = jnp.sum(attn * probs, axis=-1, keepdims=True)
        ds = (attn * (probs - inner) * scale).astype(jnp.bfloat16)
        gq_ref[:, cols] = nn(ds, k_ref[:, cols]).astype(jnp.bfloat16)
        gk_ref[:, cols] = tn(ds, q_ref[:, cols]).astype(jnp.bfloat16)


VMEM = pl.BlockSpec(memory_space=pltpu.VMEM)
SMEM = pl.BlockSpec(memory_space=pltpu.SMEM)
PARAMS = pltpu.CompilerParams(vmem_limit_bytes=24 * 1024 * 1024)


def shards(queries, attn_keys, attn_values, out_weight, grad_out):
    patches, width = queries.shape[1], queries.shape[2]
    heads = width // HD
    q, k, v = (a.reshape(patches, width) for a in (queries, attn_keys, attn_values))
    part, model = grad_out.shape[1], grad_out.shape[2]
    block = out_weight.shape[0]
    dp, mp = lax.axis_index("dp"), lax.axis_index("mp")
    core, z, y = dp % NC, (dp // NC) % NZ, dp // (NC * NZ)

    span = NZ * NC * block
    place = np.arange(span)
    z_bits = (place // block) % NZ
    z_xor = sum(((z_bits >> b) & 1) << (3 - b) for b in range(4))
    core_xor = place // (NZ * block)
    source = ((jnp.asarray(z_xor) ^ z) * NC + (jnp.asarray(core_xor) ^ core)) * block + jnp.asarray(place % block)
    pick = (jnp.arange(span)[:, None] == source[None, :]).astype(jnp.bfloat16)
    grads = jnp.dot(
        grad_out.reshape(part * NY, span), pick, preferred_element_type=jnp.float32
    ).astype(jnp.bfloat16).reshape(part, 2, 2, span)
    grads = jnp.where((y & 2) != 0, jnp.flip(grads, 1), grads)
    grads = jnp.where((y & 1) != 0, jnp.flip(grads, 2), grads)
    own = grads.reshape(part, model)

    weight = out_weight
    weight = jnp.concatenate([weight, swap(weight, z=8)], 0)
    weight = jnp.concatenate([weight, swap(weight, z=4)], 0)
    weight = jnp.concatenate([weight, swap(weight, z=2)], 0)
    weight = jnp.concatenate([weight, swap(weight, z=1)], 0)
    by_y = [weight] + [swap(weight, y=i) for i in (1, 2, 3)]
    weights = []
    for piece in by_y:
        weights += [piece, swap(piece, core=1)]

    far = swap(own, half=1)
    pieces = [own] + [swap(own, x=i) for i in (1, 2, 3)]
    pieces += [far] + [swap(far, x=i) for i in (1, 2, 3)]
    rows = jnp.stack([mp ^ (i * NH + h) for h in range(NH) for i in range(NX)]).astype(jnp.int32)

    attn = pl.pallas_call(
        attention_kernel,
        out_shape=jax.ShapeDtypeStruct((heads, patches, patches), jnp.float32),
        in_specs=[VMEM] * 2,
        out_specs=VMEM,
        compiler_params=PARAMS,
        cost_estimate=pl.CostEstimate(flops=2 * patches * patches * width, bytes_accessed=1 << 20, transcendentals=0),
    )(q, k)
    grad_shape = jax.ShapeDtypeStruct((patches, width), jnp.bfloat16)
    outs = pl.pallas_call(
        tail_kernel,
        out_shape=(grad_shape,) * 3,
        in_specs=[SMEM] + [VMEM] * (4 + len(pieces) + len(weights)),
        out_specs=(VMEM,) * 3,
        scratch_shapes=[pltpu.VMEM((patches, width), jnp.bfloat16)],
        compiler_params=PARAMS,
        cost_estimate=pl.CostEstimate(flops=2 * patches * width * (model + 4 * patches), bytes_accessed=6 << 20, transcendentals=0),
    )(rows, attn, q, k, v, *pieces, *weights)
    return tuple(o.reshape(1, patches, width) for o in outs)


def solution(mesh):
    in_specs = (
        P("dp", None, "mp"),
        P("dp", None, "mp"),
        P("dp", None, "mp"),
        P("dp", "mp"),
        P("dp", "mp", None),
    )
    out_specs = (P("dp", None, "mp"), P("dp", None, "mp"), P("dp", None, "mp"))
    return jax.shard_map(shards, mesh=mesh, in_specs=in_specs, out_specs=out_specs, check_vma=False)
```

```python
import math

import jax
import jax.numpy as jnp
import numpy as np
from jax import lax
from jax.experimental import pallas as pl
from jax.experimental.pallas import tpu as pltpu
from jax.sharding import PartitionSpec as P

HD = 128
AXES = ("dp", "mp")
NY, NZ, NC, NX, NH = 4, 16, 2, 4, 2


def exchange(y=0, z=0, core=0, x=0, half=0):
    pairs = []
    for dp in range(NY * NZ * NC):
        other = dp ^ (y * NZ * NC + z * NC + core)
        for mp in range(NX * NH):
            pairs.append((dp * NX * NH + mp, other * NX * NH + (mp ^ (x * NH + half))))
    return pairs


def swap(value, **moves):
    return lax.ppermute(value, AXES, exchange(**moves))


def after(*values):
    return lax.optimization_barrier(values)


def quarter_turn(value):
    pairs = []
    for dp in range(NY * NZ * NC):
        y, z, core = dp // (NZ * NC), dp // NC % NZ, dp % NC
        for mp in range(NX * NH):
            x, half = mp // NH, mp % NH
            ring = (half * NZ + z + (1 - 2 * core) * (NZ // 2)) % (NH * NZ)
            target = (y * NZ + ring % NZ) * NC + core
            pairs.append((dp * NX * NH + mp, target * NX * NH + x * NH + ring // NZ))
    return lax.ppermute(value, AXES, pairs)


def nt(a, b):
    return lax.dot_general(a, b, (((1,), (1,)), ((), ())), preferred_element_type=jnp.float32)


def tn(a, b):
    return lax.dot_general(a, b, (((0,), (0,)), ((), ())), preferred_element_type=jnp.float32)


def nn(a, b):
    return lax.dot_general(a, b, (((1,), (0,)), ((), ())), preferred_element_type=jnp.float32)


def reorder_kernel(y_ref, source_ref, in_ref, out_ref):
    span = source_ref.shape[1]
    wanted = lax.broadcasted_iota(jnp.int32, (span, span), 0) == source_ref[...]
    pick = jnp.where(wanted, 1.0, 0.0).astype(jnp.bfloat16)
    for i in range(NY):
        start = pl.multiple_of((y_ref[0] ^ i) * span, span)
        out_ref[:, i * span:(i + 1) * span] = nn(in_ref[:, pl.ds(start, span)], pick).astype(jnp.bfloat16)


def attention_kernel(q_ref, k_ref, out_ref):
    scale = 1.0 / math.sqrt(HD)
    for head in range(q_ref.shape[1] // HD):
        cols = pl.ds(head * HD, HD)
        scores = nt(q_ref[:, cols], k_ref[:, cols]) * scale
        raised = jnp.exp(scores - jnp.max(scores, axis=-1, keepdims=True))
        out_ref[head] = raised / jnp.sum(raised, axis=-1, keepdims=True)


def tail_kernel(rows_ref, attn_ref, q_ref, k_ref, v_ref, *refs):
    n_g = NX * NH
    n_w = NY * NC
    g_refs, w_refs = refs[:n_g], refs[n_g:n_g + n_w]
    gq_ref, gk_ref, gv_ref, grad_ref = refs[n_g + n_w:]
    scale = 1.0 / math.sqrt(HD)
    part, depth = g_refs[0].shape[0], w_refs[0].shape[0]
    total = None
    for piece in range(n_w):
        cols = pl.ds(piece * depth, depth)
        left = jnp.concatenate([g[:, cols] for g in g_refs], axis=0)
        term = nn(left, w_refs[piece][...])
        total = term if total is None else total + term
    total = total.astype(jnp.bfloat16)
    for slot in range(n_g):
        row = pl.multiple_of(rows_ref[slot] * part, part)
        grad_ref[pl.ds(row, part), :] = total[slot * part:(slot + 1) * part]
    for head in range(q_ref.shape[1] // HD):
        cols = pl.ds(head * HD, HD)
        grad = grad_ref[:, cols]
        attn = attn_ref[head]
        gv_ref[:, cols] = tn(attn.astype(jnp.bfloat16), grad).astype(jnp.bfloat16)
        probs = nt(grad, v_ref[:, cols])
        inner = jnp.sum(attn * probs, axis=-1, keepdims=True)
        ds = (attn * (probs - inner) * scale).astype(jnp.bfloat16)
        gq_ref[:, cols] = nn(ds, k_ref[:, cols]).astype(jnp.bfloat16)
        gk_ref[:, cols] = tn(ds, q_ref[:, cols]).astype(jnp.bfloat16)


VMEM = pl.BlockSpec(memory_space=pltpu.VMEM)
SMEM = pl.BlockSpec(memory_space=pltpu.SMEM)
PARAMS = pltpu.CompilerParams(vmem_limit_bytes=16 * 1024 * 1024)


def shards(queries, attn_keys, attn_values, out_weight, grad_out):
    patches, width = queries.shape[1], queries.shape[2]
    heads = width // HD
    q, k, v = (a.reshape(patches, width) for a in (queries, attn_keys, attn_values))
    part, model = grad_out.shape[1], grad_out.shape[2]
    block = out_weight.shape[0]
    dp, mp = lax.axis_index("dp"), lax.axis_index("mp")
    core, z, y = dp % NC, (dp // NC) % NZ, dp // (NC * NZ)

    span = NZ * NC * block
    place = np.arange(span)
    z_bits = (place // block) % NZ
    z_xor = sum(((z_bits >> b) & 1) << (3 - b) for b in range(4))
    core_xor = place // (NZ * block)
    source = ((jnp.asarray(z_xor) ^ z) * NC + (jnp.asarray(core_xor) ^ core)) * block + jnp.asarray(place % block)
    own = pl.pallas_call(
        reorder_kernel,
        out_shape=jax.ShapeDtypeStruct((part, model), jnp.bfloat16),
        in_specs=[SMEM, VMEM, VMEM],
        out_specs=VMEM,
        compiler_params=PARAMS,
        cost_estimate=pl.CostEstimate(flops=2 * part * model * span, bytes_accessed=4 * part * model, transcendentals=0),
    )(y.reshape(1), source.astype(jnp.int32).reshape(1, span), grad_out.reshape(part, model))

    weight = out_weight
    arrived = swap(weight, z=8)
    half_way = quarter_turn(own)
    own, arrived = after(own, arrived)
    weight = jnp.concatenate([weight, arrived], 0)
    weight = jnp.concatenate([weight, swap(weight, z=4)], 0)
    pieces = [own] + [swap(own, x=i) for i in (1, 2, 3)]
    weight, half_way = after(weight, half_way)
    far = quarter_turn(half_way)
    weight = jnp.concatenate([weight, swap(weight, z=2)], 0)
    weight = jnp.concatenate([weight, swap(weight, z=1)], 0)
    weight, far = after(weight, far)
    by_y = [weight] + [swap(weight, y=i) for i in (1, 2, 3)]
    weights = []
    for piece in by_y:
        weights += [piece, swap(piece, core=1)]
    pieces += [far] + [swap(far, x=i) for i in (1, 2, 3)]
    rows = jnp.stack([mp ^ (i * NH + h) for h in range(NH) for i in range(NX)]).astype(jnp.int32)

    attn = pl.pallas_call(
        attention_kernel,
        out_shape=jax.ShapeDtypeStruct((heads, patches, patches), jnp.float32),
        in_specs=[VMEM] * 2,
        out_specs=VMEM,
        compiler_params=PARAMS,
        cost_estimate=pl.CostEstimate(flops=2 * patches * patches * width, bytes_accessed=1 << 20, transcendentals=0),
    )(q, k)
    grad_shape = jax.ShapeDtypeStruct((patches, width), jnp.bfloat16)
    outs = pl.pallas_call(
        tail_kernel,
        out_shape=(grad_shape,) * 3,
        in_specs=[SMEM] + [VMEM] * (4 + len(pieces) + len(weights)),
        out_specs=(VMEM,) * 3,
        scratch_shapes=[pltpu.VMEM((patches, width), jnp.bfloat16)],
        compiler_params=PARAMS,
        cost_estimate=pl.CostEstimate(flops=2 * patches * width * (model + 4 * patches), bytes_accessed=6 << 20, transcendentals=0),
    )(rows, attn, q, k, v, *pieces, *weights)
    return tuple(o.reshape(1, patches, width) for o in outs)


def solution(mesh):
    in_specs = (
        P("dp", None, "mp"),
        P("dp", None, "mp"),
        P("dp", None, "mp"),
        P("dp", "mp"),
        P("dp", "mp", None),
    )
    out_specs = (P("dp", None, "mp"), P("dp", None, "mp"), P("dp", None, "mp"))
    return jax.shard_map(shards, mesh=mesh, in_specs=in_specs, out_specs=out_specs, check_vma=False)
```

```python
import math

import jax
import jax.numpy as jnp
import numpy as np
from jax import lax
from jax.experimental import pallas as pl
from jax.experimental.pallas import tpu as pltpu
from jax.sharding import PartitionSpec as P

HD = 128
AXES = ("dp", "mp")
NY, NZ, NC, NX, NH = 4, 16, 2, 4, 2
Y_ORDER = (0, 2, 1, 3)


def exchange(y=0, z=0, core=0, x=0, half=0):
    pairs = []
    for dp in range(NY * NZ * NC):
        other = dp ^ (y * NZ * NC + z * NC + core)
        for mp in range(NX * NH):
            pairs.append((dp * NX * NH + mp, other * NX * NH + (mp ^ (x * NH + half))))
    return pairs


def swap(value, **moves):
    return lax.ppermute(value, AXES, exchange(**moves))


def gather_x(value):
    groups = [[i * NH + h for i in range(NX)] for h in range(NH)]
    return lax.all_gather(value, "mp", axis_index_groups=groups, axis=0, tiled=True)


def after(*values):
    return lax.optimization_barrier(values)


def quarter_turn(value):
    pairs = []
    for dp in range(NY * NZ * NC):
        y, z, core = dp // (NZ * NC), dp // NC % NZ, dp % NC
        for mp in range(NX * NH):
            x, half = mp // NH, mp % NH
            ring = (half * NZ + z + (1 - 2 * core) * (NZ // 2)) % (NH * NZ)
            target = (y * NZ + ring % NZ) * NC + core
            pairs.append((dp * NX * NH + mp, target * NX * NH + x * NH + ring // NZ))
    return lax.ppermute(value, AXES, pairs)


def nt(a, b):
    return lax.dot_general(a, b, (((1,), (1,)), ((), ())), preferred_element_type=jnp.float32)


def tn(a, b):
    return lax.dot_general(a, b, (((0,), (0,)), ((), ())), preferred_element_type=jnp.float32)


def nn(a, b):
    return lax.dot_general(a, b, (((1,), (0,)), ((), ())), preferred_element_type=jnp.float32)


def reorder_kernel(y_ref, source_ref, in_ref, out_ref):
    span = source_ref.shape[1]
    wanted = lax.broadcasted_iota(jnp.int32, (span, span), 0) == source_ref[...]
    pick = jnp.where(wanted, 1.0, 0.0).astype(jnp.bfloat16)
    for slot, i in enumerate(Y_ORDER):
        start = pl.multiple_of((y_ref[0] ^ i) * span, span)
        out_ref[:, slot * span:(slot + 1) * span] = nn(in_ref[:, pl.ds(start, span)], pick).astype(jnp.bfloat16)


def attention_kernel(q_ref, k_ref, out_ref):
    scale = 1.0 / math.sqrt(HD)
    for head in range(q_ref.shape[1] // HD):
        cols = pl.ds(head * HD, HD)
        scores = nt(q_ref[:, cols], k_ref[:, cols]) * scale
        raised = jnp.exp(scores - jnp.max(scores, axis=-1, keepdims=True))
        out_ref[head] = raised / jnp.sum(raised, axis=-1, keepdims=True)


def tail_kernel(rows_ref, attn_ref, q_ref, k_ref, v_ref, own_ref, far_ref, w_ref, wc_ref, *refs):
    gq_ref, gk_ref, gv_ref, grad_ref = refs
    scale = 1.0 / math.sqrt(HD)
    n_g, depth = NX * NH, w_ref.shape[0] // NY
    part = q_ref.shape[0] // n_g
    parts = [ref[i * depth:(i + 1) * depth] for i in range(NY) for ref in (w_ref, wc_ref)]
    left = jnp.concatenate([own_ref[...], far_ref[...]], axis=0)
    total = None
    for i, piece in enumerate(parts):
        term = nn(left[:, i * depth:(i + 1) * depth], piece)
        total = term if total is None else total + term
    total = total.astype(jnp.bfloat16)
    for slot in range(n_g):
        row = pl.multiple_of(rows_ref[slot] * part, part)
        grad_ref[pl.ds(row, part), :] = total[slot * part:(slot + 1) * part]
    for head in range(q_ref.shape[1] // HD):
        cols = pl.ds(head * HD, HD)
        grad = grad_ref[:, cols]
        attn = attn_ref[head]
        gv_ref[:, cols] = tn(attn.astype(jnp.bfloat16), grad).astype(jnp.bfloat16)
        probs = nt(grad, v_ref[:, cols])
        inner = jnp.sum(attn * probs, axis=-1, keepdims=True)
        ds = (attn * (probs - inner) * scale).astype(jnp.bfloat16)
        gq_ref[:, cols] = nn(ds, k_ref[:, cols]).astype(jnp.bfloat16)
        gk_ref[:, cols] = tn(ds, q_ref[:, cols]).astype(jnp.bfloat16)


VMEM = pl.BlockSpec(memory_space=pltpu.VMEM)
SMEM = pl.BlockSpec(memory_space=pltpu.SMEM)
PARAMS = pltpu.CompilerParams(vmem_limit_bytes=16 * 1024 * 1024)


def shards(queries, attn_keys, attn_values, out_weight, grad_out):
    patches, width = queries.shape[1], queries.shape[2]
    heads = width // HD
    q, k, v = (a.reshape(patches, width) for a in (queries, attn_keys, attn_values))
    part, model = grad_out.shape[1], grad_out.shape[2]
    block = out_weight.shape[0]
    dp, mp = lax.axis_index("dp"), lax.axis_index("mp")
    core, z, y = dp % NC, (dp // NC) % NZ, dp // (NC * NZ)

    span = NZ * NC * block
    place = np.arange(span)
    z_bits = (place // block) % NZ
    z_xor = sum(((z_bits >> b) & 1) << (3 - b) for b in range(4))
    core_xor = place // (NZ * block)
    source = ((jnp.asarray(z_xor) ^ z) * NC + (jnp.asarray(core_xor) ^ core)) * block + jnp.asarray(place % block)
    own = pl.pallas_call(
        reorder_kernel,
        out_shape=jax.ShapeDtypeStruct((part, model), jnp.bfloat16),
        in_specs=[SMEM, VMEM, VMEM],
        out_specs=VMEM,
        compiler_params=PARAMS,
        cost_estimate=pl.CostEstimate(flops=2 * part * model * span, bytes_accessed=4 * part * model, transcendentals=0),
    )(y.reshape(1), source.astype(jnp.int32).reshape(1, span), grad_out.reshape(part, model))

    attn = pl.pallas_call(
        attention_kernel,
        out_shape=jax.ShapeDtypeStruct((heads, patches, patches), jnp.float32),
        in_specs=[VMEM] * 2,
        out_specs=VMEM,
        compiler_params=PARAMS,
        cost_estimate=pl.CostEstimate(flops=2 * patches * patches * width, bytes_accessed=1 << 20, transcendentals=0),
    )(q, k)
    weight = out_weight
    arrived = swap(weight, z=8)
    half_way = quarter_turn(own)
    own, arrived = after(own, arrived)
    weight = jnp.concatenate([weight, arrived], 0)
    weight = jnp.concatenate([weight, swap(weight, z=4)], 0)
    own = gather_x(own)
    weight, half_way, own = after(weight, half_way, own)
    far = quarter_turn(half_way)
    weight = jnp.concatenate([weight, swap(weight, z=2)], 0)
    weight = jnp.concatenate([weight, swap(weight, z=1)], 0)
    weight = jnp.concatenate([weight] + [swap(weight, y=i) for i in Y_ORDER[1:]], 0)
    far = gather_x(far)
    weight, far, attn = after(weight, far, attn)
    weights = [weight, swap(weight, core=1)]
    half = mp % NH
    rows = jnp.stack([i * NH + h for h in (half, 1 - half) for i in range(NX)]).astype(jnp.int32)

    grad_shape = jax.ShapeDtypeStruct((patches, width), jnp.bfloat16)
    outs = pl.pallas_call(
        tail_kernel,
        out_shape=(grad_shape,) * 3,
        in_specs=[SMEM] + [VMEM] * (6 + len(weights)),
        out_specs=(VMEM,) * 3,
        scratch_shapes=[pltpu.VMEM((patches, width), jnp.bfloat16)],
        compiler_params=PARAMS,
        cost_estimate=pl.CostEstimate(flops=2 * patches * width * (model + 4 * patches), bytes_accessed=6 << 20, transcendentals=0),
    )(rows, attn, q, k, v, own, far, *weights)
    return tuple(o.reshape(1, patches, width) for o in outs)


def solution(mesh):
    in_specs = (
        P("dp", None, "mp"),
        P("dp", None, "mp"),
        P("dp", None, "mp"),
        P("dp", "mp"),
        P("dp", "mp", None),
    )
    out_specs = (P("dp", None, "mp"), P("dp", None, "mp"), P("dp", None, "mp"))
    return jax.shard_map(shards, mesh=mesh, in_specs=in_specs, out_specs=out_specs, check_vma=False)
```

```python
import math

import jax
import jax.numpy as jnp
import numpy as np
from jax import lax
from jax.experimental import pallas as pl
from jax.experimental.pallas import tpu as pltpu
from jax.sharding import PartitionSpec as P

HD = 128
AXES = ("dp", "mp")
NY, NZ, NC, NX, NH = 4, 16, 2, 4, 2
Y_ORDER = (0, 2, 1, 3)
X_ORDER = (0, 2, 1, 3)


def exchange(y=0, z=0, core=0, x=0, half=0):
    pairs = []
    for dp in range(NY * NZ * NC):
        other = dp ^ (y * NZ * NC + z * NC + core)
        for mp in range(NX * NH):
            pairs.append((dp * NX * NH + mp, other * NX * NH + (mp ^ (x * NH + half))))
    return pairs


def swap(value, **moves):
    return lax.ppermute(value, AXES, exchange(**moves))


def gather_x(value):
    groups = [[i * NH + h for i in range(NX)] for h in range(NH)]
    return lax.all_gather(value, "mp", axis_index_groups=groups, axis=0, tiled=True)


def after(*values):
    return lax.optimization_barrier(values)


def quarter_turn(value):
    pairs = []
    for dp in range(NY * NZ * NC):
        y, z, core = dp // (NZ * NC), dp // NC % NZ, dp % NC
        for mp in range(NX * NH):
            x, half = mp // NH, mp % NH
            ring = (half * NZ + z + (1 - 2 * core) * (NZ // 2)) % (NH * NZ)
            target = (y * NZ + ring % NZ) * NC + core
            pairs.append((dp * NX * NH + mp, target * NX * NH + x * NH + ring // NZ))
    return lax.ppermute(value, AXES, pairs)


def nt(a, b):
    return lax.dot_general(a, b, (((1,), (1,)), ((), ())), preferred_element_type=jnp.float32)


def tn(a, b):
    return lax.dot_general(a, b, (((0,), (0,)), ((), ())), preferred_element_type=jnp.float32)


def nn(a, b):
    return lax.dot_general(a, b, (((1,), (0,)), ((), ())), preferred_element_type=jnp.float32)


def reorder_kernel(y_ref, source_ref, in_ref, out_ref, wide_ref):
    span = source_ref.shape[1]
    wanted = lax.broadcasted_iota(jnp.int32, (span, span), 0) == source_ref[...]
    pick = jnp.where(wanted, 1.0, 0.0).astype(jnp.bfloat16)
    for slot, i in enumerate(Y_ORDER):
        start = pl.multiple_of((y_ref[0] ^ i) * span, span)
        moved = nn(in_ref[:, pl.ds(start, span)], pick)
        out_ref[:, slot * span:(slot + 1) * span] = moved.astype(jnp.bfloat16)
        wide_ref[:, slot * span:(slot + 1) * span] = moved


def attention_kernel(q_ref, k_ref, out_ref):
    scale = 1.0 / math.sqrt(HD)
    for head in range(q_ref.shape[1] // HD):
        cols = pl.ds(head * HD, HD)
        scores = nt(q_ref[:, cols], k_ref[:, cols]) * scale
        raised = jnp.exp(scores - jnp.max(scores, axis=-1, keepdims=True))
        out_ref[head] = raised / jnp.sum(raised, axis=-1, keepdims=True)


def tail_kernel(rows_ref, attn_any, q_any, k_any, v_any, own_any, *refs):
    far_refs, (w_ref, wc_ref, *refs) = refs[:NX], refs[NX:]
    gq_ref, gk_ref, gv_ref, grad_ref, q_ref, k_ref, v_ref, attn_ref, own_ref, sems, own_sems = refs
    copies = [
        pltpu.make_async_copy(src, dst, sems.at[i])
        for i, (src, dst) in enumerate(((attn_any, attn_ref), (v_any, v_ref), (k_any, k_ref), (q_any, q_ref)))
    ]
    depth = w_ref.shape[0] // NY
    bands = [pl.ds(i * depth, depth) for i in range(NY * NC)]
    own_copies = [
        pltpu.make_async_copy(own_any.at[:, band], own_ref.at[:, band], own_sems.at[i])
        for i, band in enumerate(bands)
    ]
    for copy in own_copies + copies:
        copy.start()
    scale = 1.0 / math.sqrt(HD)
    n_g = NX * NH
    part = q_any.shape[0] // n_g
    parts = [ref[i * depth:(i + 1) * depth] for i in range(NY) for ref in (w_ref, wc_ref)]
    total = None
    for band, copy, piece in zip(bands, own_copies, parts):
        copy.wait()
        term = nn(jnp.concatenate([own_ref[:, band].astype(jnp.bfloat16)] + [ref[:, band] for ref in far_refs], axis=0), piece)
        total = term if total is None else total + term
    total = total.astype(jnp.bfloat16)
    for slot in range(n_g):
        row = pl.multiple_of(rows_ref[slot] * part, part)
        grad_ref[pl.ds(row, part), :] = total[slot * part:(slot + 1) * part]
    for copy in copies:
        copy.wait()
    for head in range(q_ref.shape[1] // HD):
        cols = pl.ds(head * HD, HD)
        grad = grad_ref[:, cols]
        attn = attn_ref[head]
        gv_ref[:, cols] = tn(attn.astype(jnp.bfloat16), grad).astype(jnp.bfloat16)
        probs = nt(grad, v_ref[:, cols])
        inner = jnp.sum(attn * probs, axis=-1, keepdims=True)
        ds = (attn * (probs - inner) * scale).astype(jnp.bfloat16)
        gq_ref[:, cols] = nn(ds, k_ref[:, cols]).astype(jnp.bfloat16)
        gk_ref[:, cols] = tn(ds, q_ref[:, cols]).astype(jnp.bfloat16)


VMEM = pl.BlockSpec(memory_space=pltpu.VMEM)
HBM = pl.BlockSpec(memory_space=pltpu.HBM)
SMEM = pl.BlockSpec(memory_space=pltpu.SMEM)
PARAMS = pltpu.CompilerParams(vmem_limit_bytes=16 * 1024 * 1024)


def shards(queries, attn_keys, attn_values, out_weight, grad_out):
    patches, width = queries.shape[1], queries.shape[2]
    heads = width // HD
    q, k, v = (a.reshape(patches, width) for a in (queries, attn_keys, attn_values))
    part, model = grad_out.shape[1], grad_out.shape[2]
    block = out_weight.shape[0]
    dp, mp = lax.axis_index("dp"), lax.axis_index("mp")
    core, z, y = dp % NC, (dp // NC) % NZ, dp // (NC * NZ)

    span = NZ * NC * block
    place = np.arange(span)
    z_bits = (place // block) % NZ
    z_xor = sum(((z_bits >> b) & 1) << (3 - b) for b in range(4))
    core_xor = place // (NZ * block)
    source = ((jnp.asarray(z_xor) ^ z) * NC + (jnp.asarray(core_xor) ^ core)) * block + jnp.asarray(place % block)
    own, wide = pl.pallas_call(
        reorder_kernel,
        out_shape=tuple(jax.ShapeDtypeStruct((part, model), t) for t in (jnp.bfloat16, jnp.float32)),
        in_specs=[SMEM, VMEM, VMEM],
        out_specs=(VMEM, VMEM),
        compiler_params=PARAMS,
        cost_estimate=pl.CostEstimate(flops=2 * part * model * span, bytes_accessed=4 * part * model, transcendentals=0),
    )(y.reshape(1), source.astype(jnp.int32).reshape(1, span), grad_out.reshape(part, model))

    weight = out_weight
    arrived = swap(weight, z=8)
    half_way = quarter_turn(own)
    own = gather_x(wide)
    weight = jnp.concatenate([weight, arrived], 0)
    weight = jnp.concatenate([weight, swap(weight, z=4)], 0)
    weight, half_way = after(weight, half_way)
    far = quarter_turn(half_way)
    weight = jnp.concatenate([weight, swap(weight, z=2)], 0)
    q_late, weight = after(q, weight)
    attn = pl.pallas_call(
        attention_kernel,
        out_shape=jax.ShapeDtypeStruct((heads, patches, patches), jnp.float32),
        in_specs=[VMEM] * 2,
        out_specs=VMEM,
        compiler_params=PARAMS,
        cost_estimate=pl.CostEstimate(flops=2 * patches * patches * width, bytes_accessed=1 << 20, transcendentals=0),
    )(q_late, k)
    weight = jnp.concatenate([weight, swap(weight, z=1)], 0)
    opposite = swap(weight, y=2)
    weight, far = after(weight, far)
    weight = jnp.concatenate([weight, opposite, swap(weight, y=1), swap(weight, y=3)], 0)
    far = [far] + [swap(far, x=i) for i in X_ORDER[1:]]
    weight, attn, *far = after(weight, attn, *far)
    weights = [weight, swap(weight, core=1)]
    half = mp % NH
    rows = [i * NH + half for i in range(NX)] + [mp ^ (i * NH + 1) for i in X_ORDER]
    rows = jnp.stack(rows).astype(jnp.int32)

    grad_shape = jax.ShapeDtypeStruct((patches, width), jnp.bfloat16)
    outs = pl.pallas_call(
        tail_kernel,
        out_shape=(grad_shape,) * 3,
        in_specs=[SMEM, HBM] + [HBM] * 4 + [VMEM] * (len(far) + len(weights)),
        out_specs=(VMEM,) * 3,
        scratch_shapes=[pltpu.VMEM((patches, width), jnp.bfloat16)] * 4
        + [pltpu.VMEM(a.shape, a.dtype) for a in (attn, own)]
        + [pltpu.SemaphoreType.DMA((4,)), pltpu.SemaphoreType.DMA((NY * NC,))],
        compiler_params=PARAMS,
        cost_estimate=pl.CostEstimate(flops=2 * patches * width * (model + 4 * patches), bytes_accessed=6 << 20, transcendentals=0),
    )(rows, attn, q, k, v, own, *far, *weights)
    return tuple(o.reshape(1, patches, width) for o in outs)


def solution(mesh):
    in_specs = (
        P("dp", None, "mp"),
        P("dp", None, "mp"),
        P("dp", None, "mp"),
        P("dp", "mp"),
        P("dp", "mp", None),
    )
    out_specs = (P("dp", None, "mp"), P("dp", None, "mp"), P("dp", None, "mp"))
    return jax.shard_map(shards, mesh=mesh, in_specs=in_specs, out_specs=out_specs, check_vma=False)
```

```python
import math

import jax
import jax.numpy as jnp
from jax import lax
from jax.experimental import pallas as pl
from jax.experimental.pallas import tpu as pltpu
from jax.sharding import PartitionSpec as P

HD = 128
AXES = ("dp", "mp")
NY, NZ, NC, NX, NH = 4, 16, 2, 4, 2
Y_ORDER = (0, 2, 1, 3)


def exchange(y=0, z=0, core=0, x=0, half=0):
    pairs = []
    for dp in range(NY * NZ * NC):
        other = dp ^ (y * NZ * NC + z * NC + core)
        for mp in range(NX * NH):
            pairs.append((dp * NX * NH + mp, other * NX * NH + (mp ^ (x * NH + half))))
    return pairs


def swap(value, **moves):
    return lax.ppermute(value, AXES, exchange(**moves))


def gather_x(value):
    groups = [[i * NH + h for i in range(NX)] for h in range(NH)]
    return lax.all_gather(value, "mp", axis_index_groups=groups, axis=0, tiled=True)


def share_quad(value):
    groups = [
        [((y * NZ) + quad * 4 + i) * NC + core for i in range(4)]
        for y in range(NY) for quad in range(NZ // 4) for core in range(NC)
    ]
    copies = jnp.broadcast_to(value[None], (4,) + value.shape)
    shared = lax.all_to_all(copies, "dp", 0, 0, axis_index_groups=groups)
    return shared.reshape(4 * value.shape[0], value.shape[1])


def after(*values):
    return lax.optimization_barrier(values)


def quarter_turn(value):
    pairs = []
    for dp in range(NY * NZ * NC):
        y, z, core = dp // (NZ * NC), dp // NC % NZ, dp % NC
        for mp in range(NX * NH):
            x, half = mp // NH, mp % NH
            ring = (half * NZ + z + (1 - 2 * core) * (NZ // 2)) % (NH * NZ)
            target = (y * NZ + ring % NZ) * NC + core
            pairs.append((dp * NX * NH + mp, target * NX * NH + x * NH + ring // NZ))
    return lax.ppermute(value, AXES, pairs)


def nt(a, b):
    return lax.dot_general(a, b, (((1,), (1,)), ((), ())), preferred_element_type=jnp.float32)


def tn(a, b):
    return lax.dot_general(a, b, (((0,), (0,)), ((), ())), preferred_element_type=jnp.float32)


def nn(a, b):
    return lax.dot_general(a, b, (((1,), (0,)), ((), ())), preferred_element_type=jnp.float32)


def reorder_kernel(at_ref, in_any, out_ref, in_ref, sem):
    load = pltpu.make_async_copy(in_any, in_ref, sem)
    load.start()
    span = in_ref.shape[1] // NY
    block = span // (NZ * NC)
    y, z, core = at_ref[0], at_ref[1], at_ref[2]
    place = lax.broadcasted_iota(jnp.int32, (8, span), 1)
    half = sum((place >= i * NZ * block).astype(jnp.int32) for i in range(1, NC))
    slot = sum((place >= i * block).astype(jnp.int32) for i in range(1, NC * NZ))
    inside = place - slot * block
    slot = slot & (NZ - 1)
    quad = ((slot & 1) << 3) | ((slot & 2) << 1)
    source = (((quad ^ (z & 12)) | (slot >> 2)) * NC + (half ^ core)) * block + inside
    wanted = lax.broadcasted_iota(jnp.int32, (span, span), 0) == source[0:1]
    pick = jnp.where(wanted, 1.0, 0.0).astype(jnp.bfloat16)
    load.wait()
    for slot, i in enumerate(Y_ORDER):
        start = pl.multiple_of((y ^ i) * span, span)
        out_ref[:, slot * span:(slot + 1) * span] = nn(in_ref[:, pl.ds(start, span)], pick).astype(jnp.bfloat16)


def attention_kernel(q_ref, k_ref, out_ref):
    scale = 1.0 / math.sqrt(HD)
    for head in range(q_ref.shape[1] // HD):
        cols = pl.ds(head * HD, HD)
        scores = nt(q_ref[:, cols], k_ref[:, cols]) * scale
        raised = jnp.exp(scores - jnp.max(scores, axis=-1, keepdims=True))
        out_ref[head] = raised / jnp.sum(raised, axis=-1, keepdims=True)


def tail_kernel(rows_ref, attn_ref, w_ref, wc_ref, q_any, k_any, v_any, own_any, far_any, *refs):
    gq_ref, gk_ref, gv_ref, grad_ref, q_ref, k_ref, v_ref, g_ref, sems, band_sems = refs
    scale = 1.0 / math.sqrt(HD)
    n_g = NX * NH
    part = q_ref.shape[0] // n_g
    rows, depth = own_any.shape[0], w_ref.shape[0] // NY
    band_copies = []
    for i in range(NY):
        band = pl.ds(i * NC * depth, NC * depth)
        pairs = (
            (own_any.at[:, band], g_ref.at[:rows, band]),
            (far_any.at[:, band], g_ref.at[rows:, band]),
        )
        band_copies.append([pltpu.make_async_copy(*pair, band_sems.at[i, j]) for j, pair in enumerate(pairs)])
    copies = [
        pltpu.make_async_copy(src, dst, sems.at[i])
        for i, (src, dst) in enumerate(((v_any, v_ref), (k_any, k_ref), (q_any, q_ref)))
    ]
    for copy in sum(band_copies, []) + copies:
        copy.start()
    weights = [ref[i * depth:(i + 1) * depth] for i in range(NY) for ref in (w_ref, wc_ref)]
    total = None
    for i in range(NY * NC):
        if i % NC == 0:
            for copy in band_copies[i // NC]:
                copy.wait()
        term = nn(g_ref[:, i * depth:(i + 1) * depth], weights[i])
        total = term if total is None else total + term
    for copy in copies:
        copy.wait()
    total = total.astype(jnp.bfloat16)
    for slot in range(n_g):
        row = pl.multiple_of(rows_ref[slot] * part, part)
        grad_ref[pl.ds(row, part), :] = total[slot * part:(slot + 1) * part]
    for head in range(q_ref.shape[1] // HD):
        cols = pl.ds(head * HD, HD)
        grad = grad_ref[:, cols]
        attn = attn_ref[head]
        gv_ref[:, cols] = tn(attn.astype(jnp.bfloat16), grad).astype(jnp.bfloat16)
        probs = nt(grad, v_ref[:, cols])
        inner = jnp.sum(attn * probs, axis=-1, keepdims=True)
        ds = (attn * (probs - inner) * scale).astype(jnp.bfloat16)
        gq_ref[:, cols] = nn(ds, k_ref[:, cols]).astype(jnp.bfloat16)
        gk_ref[:, cols] = tn(ds, q_ref[:, cols]).astype(jnp.bfloat16)


VMEM = pl.BlockSpec(memory_space=pltpu.VMEM)
ANY = pl.BlockSpec(memory_space=pl.ANY)
TAIL_VMEM = 52 * 1024 * 1024
SMEM = pl.BlockSpec(memory_space=pltpu.SMEM)
PARAMS = pltpu.CompilerParams(vmem_limit_bytes=16 * 1024 * 1024)


def shards(queries, attn_keys, attn_values, out_weight, grad_out):
    patches, width = queries.shape[1], queries.shape[2]
    heads = width // HD
    q, k, v = (a.reshape(patches, width) for a in (queries, attn_keys, attn_values))
    part, model = grad_out.shape[1], grad_out.shape[2]
    dp, mp = lax.axis_index("dp"), lax.axis_index("mp")
    core, z, y = dp % NC, (dp // NC) % NZ, dp // (NC * NZ)

    own = pl.pallas_call(
        reorder_kernel,
        out_shape=jax.ShapeDtypeStruct((part, model), jnp.bfloat16),
        in_specs=[SMEM, ANY],
        out_specs=VMEM,
        scratch_shapes=[pltpu.VMEM((part, model), jnp.bfloat16), pltpu.SemaphoreType.DMA],
        compiler_params=PARAMS,
        cost_estimate=pl.CostEstimate(flops=2 * part * model * model // NY, bytes_accessed=4 * part * model, transcendentals=0),
    )(jnp.stack([y, z, core]).astype(jnp.int32), grad_out.reshape(part, model))

    attn = pl.pallas_call(
        attention_kernel,
        out_shape=jax.ShapeDtypeStruct((heads, patches, patches), jnp.float32),
        in_specs=[VMEM] * 2,
        out_specs=VMEM,
        compiler_params=PARAMS,
        cost_estimate=pl.CostEstimate(flops=2 * patches * patches * width, bytes_accessed=1 << 20, transcendentals=0),
    )(q, k)
    weight = out_weight
    arrived = swap(weight, z=8)
    half_way = quarter_turn(own)
    own, arrived = after(own, arrived)
    weight = jnp.concatenate([weight, arrived], 0)
    weight = jnp.concatenate([weight, swap(weight, z=4)], 0)
    own = gather_x(own)
    weight, half_way, own = after(weight, half_way, own)
    far = quarter_turn(half_way)
    weight = share_quad(weight)
    weight = jnp.concatenate([weight] + [swap(weight, y=i) for i in Y_ORDER[1:]], 0)
    far = gather_x(far)
    weight, far, attn = after(weight, far, attn)
    weights = [weight, swap(weight, core=1)]
    half = mp % NH
    rows = jnp.stack([i * NH + h for h in (half, 1 - half) for i in range(NX)]).astype(jnp.int32)

    grad_shape = jax.ShapeDtypeStruct((patches, width), jnp.bfloat16)
    outs = pl.pallas_call(
        tail_kernel,
        out_shape=(grad_shape,) * 3,
        in_specs=[SMEM] + [VMEM] * 3 + [ANY] * 5,
        out_specs=(VMEM,) * 3,
        scratch_shapes=[
            pltpu.VMEM((patches, width), jnp.bfloat16),
            *[pltpu.VMEM((patches, width), jnp.bfloat16)] * 3,
            pltpu.VMEM((patches, model), jnp.bfloat16),
            pltpu.SemaphoreType.DMA((3,)),
            pltpu.SemaphoreType.DMA((NY, 2)),
        ],
        compiler_params=pltpu.CompilerParams(vmem_limit_bytes=TAIL_VMEM),
        cost_estimate=pl.CostEstimate(flops=2 * patches * width * (model + 4 * patches), bytes_accessed=6 << 20, transcendentals=0),
    )(rows, attn, *weights, q, k, v, own, far)
    return tuple(o.reshape(1, patches, width) for o in outs)


def solution(mesh):
    in_specs = (
        P("dp", None, "mp"),
        P("dp", None, "mp"),
        P("dp", None, "mp"),
        P("dp", "mp"),
        P("dp", "mp", None),
    )
    out_specs = (P("dp", None, "mp"), P("dp", None, "mp"), P("dp", None, "mp"))
    return jax.shard_map(shards, mesh=mesh, in_specs=in_specs, out_specs=out_specs, check_vma=False)
```

```python
import math

import jax
import jax.numpy as jnp
from jax import lax
from jax.experimental import pallas as pl
from jax.experimental.pallas import tpu as pltpu
from jax.sharding import PartitionSpec as P

HD = 128
AXES = ("dp", "mp")
NY, NZ, NC, NX, NH = 4, 16, 2, 4, 2


def exchange(y=0, z=0, core=0, x=0, half=0):
    pairs = []
    for dp in range(NY * NZ * NC):
        other = dp ^ (y * NZ * NC + z * NC + core)
        for mp in range(NX * NH):
            pairs.append((dp * NX * NH + mp, other * NX * NH + (mp ^ (x * NH + half))))
    return pairs


def swap(value, **moves):
    return lax.ppermute(value, AXES, exchange(**moves))


def share(value, axis, groups):
    copies = jnp.broadcast_to(value[None], (len(groups[0]),) + value.shape)
    shared = lax.all_to_all(copies, axis, 0, 0, axis_index_groups=groups)
    return shared.reshape(-1, value.shape[1])


def dp_index(y, z, core):
    return (y * NZ + z) * NC + core


X_GROUPS = [[x * NH + half for x in range(NX)] for half in range(NH)]
Y_GROUPS = [[dp_index(y, z, core) for y in range(NY)] for z in range(NZ) for core in range(NC)]
NEAR_GROUPS = [
    [dp_index(y, quad * 4 + i, core) for i in range(4)]
    for y in range(NY) for quad in range(4) for core in range(NC)
]
FAR_GROUPS = [
    [dp_index(y, quad * 4 + i, core) for quad in range(4)]
    for y in range(NY) for i in range(4) for core in range(NC)
]


def after(*values):
    return lax.optimization_barrier(values)


def quarter_turn(value):
    pairs = []
    for dp in range(NY * NZ * NC):
        y, z, core = dp // (NZ * NC), dp // NC % NZ, dp % NC
        for mp in range(NX * NH):
            x, half = mp // NH, mp % NH
            ring = (half * NZ + z + (1 - 2 * core) * (NZ // 2)) % (NH * NZ)
            target = (y * NZ + ring % NZ) * NC + core
            pairs.append((dp * NX * NH + mp, target * NX * NH + x * NH + ring // NZ))
    return lax.ppermute(value, AXES, pairs)


def nt(a, b):
    return lax.dot_general(a, b, (((1,), (1,)), ((), ())), preferred_element_type=jnp.float32)


def tn(a, b):
    return lax.dot_general(a, b, (((0,), (0,)), ((), ())), preferred_element_type=jnp.float32)


def nn(a, b):
    return lax.dot_general(a, b, (((1,), (0,)), ((), ())), preferred_element_type=jnp.float32)


def reorder_kernel(core_ref, in_any, out_ref, in_ref, sem):
    load = pltpu.make_async_copy(in_any, in_ref, sem)
    load.start()
    span = in_ref.shape[1] // NY
    block = span // (NZ * NC)
    place = lax.broadcasted_iota(jnp.int32, (8, span), 1)
    half = sum((place >= i * NZ * block).astype(jnp.int32) for i in range(1, NC))
    slot = sum((place >= i * block).astype(jnp.int32) for i in range(1, NC * NZ))
    inside = place - slot * block
    slot = slot & (NZ - 1)
    z = ((slot & 3) << 2) | (slot >> 2)
    source = (z * NC + (half ^ core_ref[0])) * block + inside
    wanted = lax.broadcasted_iota(jnp.int32, (span, span), 0) == source[0:1]
    pick = jnp.where(wanted, 1.0, 0.0).astype(jnp.bfloat16)
    load.wait()
    for i in range(NY):
        cols = pl.ds(i * span, span)
        out_ref[:, cols] = nn(in_ref[:, cols], pick).astype(jnp.bfloat16)


def attention_kernel(q_ref, k_ref, out_ref):
    scale = 1.0 / math.sqrt(HD)
    for head in range(q_ref.shape[1] // HD):
        cols = pl.ds(head * HD, HD)
        scores = nt(q_ref[:, cols], k_ref[:, cols]) * scale
        raised = jnp.exp(scores - jnp.max(scores, axis=-1, keepdims=True))
        out_ref[head] = raised / jnp.sum(raised, axis=-1, keepdims=True)


def tail_kernel(rows_ref, attn_ref, w_ref, wc_ref, q_any, k_any, v_any, own_any, far_any, *refs):
    gq_ref, gk_ref, gv_ref, grad_ref, q_ref, k_ref, v_ref, g_ref, sems, band_sems = refs
    scale = 1.0 / math.sqrt(HD)
    n_g = NX * NH
    part = q_ref.shape[0] // n_g
    rows, depth = own_any.shape[0], w_ref.shape[0] // NY
    band_copies = []
    for i in range(NY):
        band = pl.ds(i * NC * depth, NC * depth)
        pairs = (
            (own_any.at[:, band], g_ref.at[:rows, band]),
            (far_any.at[:, band], g_ref.at[rows:, band]),
        )
        band_copies.append([pltpu.make_async_copy(*pair, band_sems.at[i, j]) for j, pair in enumerate(pairs)])
    copies = [
        pltpu.make_async_copy(src, dst, sems.at[i])
        for i, (src, dst) in enumerate(((v_any, v_ref), (k_any, k_ref), (q_any, q_ref)))
    ]
    for copy in sum(band_copies, []) + copies:
        copy.start()
    weights = [ref[i * depth:(i + 1) * depth] for i in range(NY) for ref in (w_ref, wc_ref)]
    total = None
    for i in range(NY * NC):
        if i % NC == 0:
            for copy in band_copies[i // NC]:
                copy.wait()
        term = nn(g_ref[:, i * depth:(i + 1) * depth], weights[i])
        total = term if total is None else total + term
    for copy in copies:
        copy.wait()
    total = total.astype(jnp.bfloat16)
    for slot in range(n_g):
        row = pl.multiple_of(rows_ref[slot] * part, part)
        grad_ref[pl.ds(row, part), :] = total[slot * part:(slot + 1) * part]
    for head in range(q_ref.shape[1] // HD):
        cols = pl.ds(head * HD, HD)
        grad = grad_ref[:, cols]
        attn = attn_ref[head]
        gv_ref[:, cols] = tn(attn.astype(jnp.bfloat16), grad).astype(jnp.bfloat16)
        probs = nt(grad, v_ref[:, cols])
        inner = jnp.sum(attn * probs, axis=-1, keepdims=True)
        ds = (attn * (probs - inner) * scale).astype(jnp.bfloat16)
        gq_ref[:, cols] = nn(ds, k_ref[:, cols]).astype(jnp.bfloat16)
        gk_ref[:, cols] = tn(ds, q_ref[:, cols]).astype(jnp.bfloat16)


VMEM = pl.BlockSpec(memory_space=pltpu.VMEM)
ANY = pl.BlockSpec(memory_space=pl.ANY)
ATTENTION_HINT = 8 * 10**9
TAIL_VMEM = 52 * 1024 * 1024
SMEM = pl.BlockSpec(memory_space=pltpu.SMEM)
PARAMS = pltpu.CompilerParams(vmem_limit_bytes=16 * 1024 * 1024)


def shards(queries, attn_keys, attn_values, out_weight, grad_out):
    patches, width = queries.shape[1], queries.shape[2]
    heads = width // HD
    q, k, v = (a.reshape(patches, width) for a in (queries, attn_keys, attn_values))
    part, model = grad_out.shape[1], grad_out.shape[2]
    dp, mp = lax.axis_index("dp"), lax.axis_index("mp")

    own = pl.pallas_call(
        reorder_kernel,
        out_shape=jax.ShapeDtypeStruct((part, model), jnp.bfloat16),
        in_specs=[SMEM, ANY],
        out_specs=VMEM,
        scratch_shapes=[pltpu.VMEM((part, model), jnp.bfloat16), pltpu.SemaphoreType.DMA],
        compiler_params=PARAMS,
        cost_estimate=pl.CostEstimate(flops=2 * part * model * model // NY, bytes_accessed=4 * part * model, transcendentals=0),
    )((dp % NC).astype(jnp.int32).reshape(1), grad_out.reshape(part, model))

    weight = share(out_weight, "dp", FAR_GROUPS)
    half_way = quarter_turn(own)
    own = lax.all_gather(own, "mp", axis_index_groups=X_GROUPS, axis=0, tiled=True)
    weight, half_way, own = after(weight, half_way, own)
    weight = share(weight, "dp", NEAR_GROUPS)
    far = quarter_turn(half_way)
    weight = share(weight, "dp", Y_GROUPS)
    q_late, far = after(q, far)
    attn = pl.pallas_call(
        attention_kernel,
        out_shape=jax.ShapeDtypeStruct((heads, patches, patches), jnp.float32),
        in_specs=[VMEM] * 2,
        out_specs=VMEM,
        compiler_params=PARAMS,
        cost_estimate=pl.CostEstimate(flops=ATTENTION_HINT, bytes_accessed=1 << 20, transcendentals=0),
    )(q_late, k)
    weight, far, attn = after(weight, far, attn)
    far = share(far, "mp", X_GROUPS)
    weights = [weight, swap(weight, core=1)]
    half = mp % NH
    rows = jnp.stack([i * NH + h for h in (half, 1 - half) for i in range(NX)]).astype(jnp.int32)

    grad_shape = jax.ShapeDtypeStruct((patches, width), jnp.bfloat16)
    outs = pl.pallas_call(
        tail_kernel,
        out_shape=(grad_shape,) * 3,
        in_specs=[SMEM] + [VMEM] * 3 + [ANY] * 5,
        out_specs=(VMEM,) * 3,
        scratch_shapes=[
            pltpu.VMEM((patches, width), jnp.bfloat16),
            *[pltpu.VMEM((patches, width), jnp.bfloat16)] * 3,
            pltpu.VMEM((patches, model), jnp.bfloat16),
            pltpu.SemaphoreType.DMA((3,)),
            pltpu.SemaphoreType.DMA((NY, 2)),
        ],
        compiler_params=pltpu.CompilerParams(vmem_limit_bytes=TAIL_VMEM),
        cost_estimate=pl.CostEstimate(flops=2 * patches * width * (model + 4 * patches), bytes_accessed=6 << 20, transcendentals=0),
    )(rows, attn, *weights, q, k, v, own, far)
    return tuple(o.reshape(1, patches, width) for o in outs)


def solution(mesh):
    in_specs = (
        P("dp", None, "mp"),
        P("dp", None, "mp"),
        P("dp", None, "mp"),
        P("dp", "mp"),
        P("dp", "mp", None),
    )
    out_specs = (P("dp", None, "mp"), P("dp", None, "mp"), P("dp", None, "mp"))
    return jax.shard_map(shards, mesh=mesh, in_specs=in_specs, out_specs=out_specs, check_vma=False)
```

```python
import math

import jax
import jax.numpy as jnp
from jax import lax
from jax.experimental import pallas as pl
from jax.experimental.pallas import tpu as pltpu
from jax.sharding import PartitionSpec as P

HD = 128
AXES = ("dp", "mp")
NY, NZ, NC, NX, NH = 4, 16, 2, 4, 2
X_ORDER = (0, 2, 1, 3)


def exchange(y=0, z=0, core=0, x=0, half=0):
    pairs = []
    for dp in range(NY * NZ * NC):
        other = dp ^ (y * NZ * NC + z * NC + core)
        for mp in range(NX * NH):
            pairs.append((dp * NX * NH + mp, other * NX * NH + (mp ^ (x * NH + half))))
    return pairs


def swap(value, **moves):
    return lax.ppermute(value, AXES, exchange(**moves))


def share(value, axis, groups):
    copies = jnp.broadcast_to(value[None], (len(groups[0]),) + value.shape)
    shared = lax.all_to_all(copies, axis, 0, 0, axis_index_groups=groups)
    return shared.reshape(-1, value.shape[1])


def dp_index(y, z, core):
    return (y * NZ + z) * NC + core


X_GROUPS = [[x * NH + half for x in range(NX)] for half in range(NH)]
Y_GROUPS = [[dp_index(y, z, core) for y in range(NY)] for z in range(NZ) for core in range(NC)]
NEAR_GROUPS = [
    [dp_index(y, quad * 4 + i, core) for i in range(4)]
    for y in range(NY) for quad in range(4) for core in range(NC)
]


def after(*values):
    return lax.optimization_barrier(values)


def quarter_turn(value):
    pairs = []
    for dp in range(NY * NZ * NC):
        y, z, core = dp // (NZ * NC), dp // NC % NZ, dp % NC
        for mp in range(NX * NH):
            x, half = mp // NH, mp % NH
            ring = (half * NZ + z + (1 - 2 * core) * (NZ // 2)) % (NH * NZ)
            target = (y * NZ + ring % NZ) * NC + core
            pairs.append((dp * NX * NH + mp, target * NX * NH + x * NH + ring // NZ))
    return lax.ppermute(value, AXES, pairs)


def nt(a, b):
    return lax.dot_general(a, b, (((1,), (1,)), ((), ())), preferred_element_type=jnp.float32)


def tn(a, b):
    return lax.dot_general(a, b, (((0,), (0,)), ((), ())), preferred_element_type=jnp.float32)


def nn(a, b):
    return lax.dot_general(a, b, (((1,), (0,)), ((), ())), preferred_element_type=jnp.float32)


def reorder_kernel(at_ref, in_any, out_ref, in_ref, sem):
    load = pltpu.make_async_copy(in_any, in_ref, sem)
    load.start()
    span = in_ref.shape[1] // NY
    block = span // (NZ * NC)
    z, core = at_ref[0], at_ref[1]
    place = lax.broadcasted_iota(jnp.int32, (8, span), 1)
    half = sum((place >= i * NZ * block).astype(jnp.int32) for i in range(1, NC))
    slot = sum((place >= i * block).astype(jnp.int32) for i in range(1, NC * NZ))
    inside = place - slot * block
    slot = slot & (NZ - 1)
    quad = ((slot & 1) << 3) | ((slot & 2) << 1)
    source = (((quad ^ (z & 12)) | (slot >> 2)) * NC + (half ^ core)) * block + inside
    wanted = lax.broadcasted_iota(jnp.int32, (span, span), 0) == source[0:1]
    pick = jnp.where(wanted, 1.0, 0.0).astype(jnp.bfloat16)
    load.wait()
    for i in range(NY):
        cols = pl.ds(i * span, span)
        out_ref[:, cols] = nn(in_ref[:, cols], pick).astype(jnp.bfloat16)


def attention_kernel(q_ref, k_ref, out_ref):
    scale = 1.0 / math.sqrt(HD)
    for head in range(q_ref.shape[1] // HD):
        cols = pl.ds(head * HD, HD)
        scores = nt(q_ref[:, cols], k_ref[:, cols]) * scale
        raised = jnp.exp(scores - jnp.max(scores, axis=-1, keepdims=True))
        out_ref[head] = raised / jnp.sum(raised, axis=-1, keepdims=True)


def tail_kernel(rows_ref, attn_ref, w_ref, wc_ref, own_ref, *refs):
    far_refs, (q_any, k_any, v_any, *refs) = refs[:NX], refs[NX:]
    gq_ref, gk_ref, gv_ref, grad_ref, q_ref, k_ref, v_ref, sems = refs
    scale = 1.0 / math.sqrt(HD)
    n_g = NX * NH
    part, depth = far_refs[0].shape[0], w_ref.shape[0] // NY
    copies = [
        pltpu.make_async_copy(src, dst, sems.at[i])
        for i, (src, dst) in enumerate(((v_any, v_ref), (k_any, k_ref), (q_any, q_ref)))
    ]
    for copy in copies:
        copy.start()
    weights = [ref[i * depth:(i + 1) * depth] for i in range(NY) for ref in (w_ref, wc_ref)]
    total = None
    for i in range(NY * NC):
        band = pl.ds(i * depth, depth)
        left = jnp.concatenate([ref[:, band] for ref in (own_ref, *far_refs)], axis=0)
        term = nn(left, weights[i])
        total = term if total is None else total + term
    for copy in copies:
        copy.wait()
    total = total.astype(jnp.bfloat16)
    for slot in range(n_g):
        row = pl.multiple_of(rows_ref[slot] * part, part)
        grad_ref[pl.ds(row, part), :] = total[slot * part:(slot + 1) * part]
    for head in range(q_ref.shape[1] // HD):
        cols = pl.ds(head * HD, HD)
        grad = grad_ref[:, cols]
        attn = attn_ref[head]
        gv_ref[:, cols] = tn(attn.astype(jnp.bfloat16), grad).astype(jnp.bfloat16)
        probs = nt(grad, v_ref[:, cols])
        inner = jnp.sum(attn * probs, axis=-1, keepdims=True)
        ds = (attn * (probs - inner) * scale).astype(jnp.bfloat16)
        gq_ref[:, cols] = nn(ds, k_ref[:, cols]).astype(jnp.bfloat16)
        gk_ref[:, cols] = tn(ds, q_ref[:, cols]).astype(jnp.bfloat16)


VMEM = pl.BlockSpec(memory_space=pltpu.VMEM)
ANY = pl.BlockSpec(memory_space=pl.ANY)
ATTENTION_HINT = 8 * 10**9
TAIL_VMEM = 40 * 1024 * 1024
REORDER_VMEM = 60 * 1024 * 1024
SMEM = pl.BlockSpec(memory_space=pltpu.SMEM)
PARAMS = pltpu.CompilerParams(vmem_limit_bytes=16 * 1024 * 1024)


def shards(queries, attn_keys, attn_values, out_weight, grad_out):
    patches, width = queries.shape[1], queries.shape[2]
    heads = width // HD
    q, k, v = (a.reshape(patches, width) for a in (queries, attn_keys, attn_values))
    part, model = grad_out.shape[1], grad_out.shape[2]
    dp, mp = lax.axis_index("dp"), lax.axis_index("mp")
    core, z = dp % NC, (dp // NC) % NZ

    own = pl.pallas_call(
        reorder_kernel,
        out_shape=jax.ShapeDtypeStruct((part, model), jnp.bfloat16),
        in_specs=[SMEM, ANY],
        out_specs=VMEM,
        scratch_shapes=[pltpu.VMEM((part, model), jnp.bfloat16), pltpu.SemaphoreType.DMA],
        compiler_params=pltpu.CompilerParams(vmem_limit_bytes=REORDER_VMEM),
        cost_estimate=pl.CostEstimate(flops=2 * part * model * model // NY, bytes_accessed=4 * part * model, transcendentals=0),
    )(jnp.stack([z, core]).astype(jnp.int32), grad_out.reshape(part, model))

    weight = out_weight
    arrived = swap(weight, z=8)
    half_way = quarter_turn(own)
    own, arrived = after(own, arrived)
    weight = jnp.concatenate([weight, arrived], 0)
    weight = jnp.concatenate([weight, swap(weight, z=4)], 0)
    own = lax.all_gather(own, "mp", axis_index_groups=X_GROUPS, axis=0, tiled=True)
    weight, half_way, own = after(weight, half_way, own)
    weight = share(weight, "dp", NEAR_GROUPS)
    far = quarter_turn(half_way)
    weight = share(weight, "dp", Y_GROUPS)
    q_late, far = after(q, far)
    attn = pl.pallas_call(
        attention_kernel,
        out_shape=jax.ShapeDtypeStruct((heads, patches, patches), jnp.float32),
        in_specs=[VMEM] * 2,
        out_specs=VMEM,
        compiler_params=PARAMS,
        cost_estimate=pl.CostEstimate(flops=ATTENTION_HINT, bytes_accessed=1 << 20, transcendentals=0),
    )(q_late, k)
    weight, attn, far = after(weight, attn, far)
    far = [far] + [swap(far, x=i) for i in X_ORDER[1:]]
    weights = [weight, swap(weight, core=1)]
    half = mp % NH
    rows = [i * NH + half for i in range(NX)] + [mp ^ (i * NH + 1) for i in X_ORDER]
    rows = jnp.stack(rows).astype(jnp.int32)

    grad_shape = jax.ShapeDtypeStruct((patches, width), jnp.bfloat16)
    outs = pl.pallas_call(
        tail_kernel,
        out_shape=(grad_shape,) * 3,
        in_specs=[SMEM] + [VMEM] * (4 + len(far)) + [ANY] * 3,
        out_specs=(VMEM,) * 3,
        scratch_shapes=[
            pltpu.VMEM((patches, width), jnp.bfloat16),
            *[pltpu.VMEM((patches, width), jnp.bfloat16)] * 3,
            pltpu.SemaphoreType.DMA((3,)),
        ],
        compiler_params=pltpu.CompilerParams(vmem_limit_bytes=TAIL_VMEM),
        cost_estimate=pl.CostEstimate(flops=2 * patches * width * (model + 4 * patches), bytes_accessed=6 << 20, transcendentals=0),
    )(rows, attn, *weights, own, *far, q, k, v)
    return tuple(o.reshape(1, patches, width) for o in outs)


def solution(mesh):
    in_specs = (
        P("dp", None, "mp"),
        P("dp", None, "mp"),
        P("dp", None, "mp"),
        P("dp", "mp"),
        P("dp", "mp", None),
    )
    out_specs = (P("dp", None, "mp"), P("dp", None, "mp"), P("dp", None, "mp"))
    return jax.shard_map(shards, mesh=mesh, in_specs=in_specs, out_specs=out_specs, check_vma=False)
```

```python
import math

import jax
import jax.numpy as jnp
import numpy as np
from jax import lax
from jax.experimental import pallas as pl
from jax.experimental.pallas import tpu as pltpu
from jax.sharding import PartitionSpec as P

HD = 128
AXES = ("dp", "mp")
NY, NZ, NC, NX, NH = 4, 16, 2, 4, 2


def exchange(y=0, z=0, core=0, x=0, half=0):
    pairs = []
    for dp in range(NY * NZ * NC):
        other = dp ^ (y * NZ * NC + z * NC + core)
        for mp in range(NX * NH):
            pairs.append((dp * NX * NH + mp, other * NX * NH + (mp ^ (x * NH + half))))
    return pairs


def swap(value, **moves):
    return lax.ppermute(value, AXES, exchange(**moves))


def gather_x(value):
    groups = [[i * NH + h for i in range(NX)] for h in range(NH)]
    return lax.all_gather(value, "mp", axis_index_groups=groups, axis=0, tiled=True)


def share_quads(value):
    groups = [
        [(y * NZ + quad * 4 + i) * NC + core for y in range(NY) for i in range(4)]
        for quad in range(NZ // 4) for core in range(NC)
    ]
    copies = jnp.broadcast_to(value[None], (NY * 4,) + value.shape)
    shared = lax.all_to_all(copies, "dp", 0, 0, axis_index_groups=groups)
    return shared.reshape(-1, value.shape[1])


def after(*values):
    return lax.optimization_barrier(values)


def quarter_turn(value):
    pairs = []
    for dp in range(NY * NZ * NC):
        y, z, core = dp // (NZ * NC), dp // NC % NZ, dp % NC
        for mp in range(NX * NH):
            x, half = mp // NH, mp % NH
            ring = (half * NZ + z + (1 - 2 * core) * (NZ // 2)) % (NH * NZ)
            target = (y * NZ + ring % NZ) * NC + core
            pairs.append((dp * NX * NH + mp, target * NX * NH + x * NH + ring // NZ))
    return lax.ppermute(value, AXES, pairs)


def nt(a, b):
    return lax.dot_general(a, b, (((1,), (1,)), ((), ())), preferred_element_type=jnp.float32)


def tn(a, b):
    return lax.dot_general(a, b, (((0,), (0,)), ((), ())), preferred_element_type=jnp.float32)


def nn(a, b):
    return lax.dot_general(a, b, (((1,), (0,)), ((), ())), preferred_element_type=jnp.float32)


def reorder_kernel(source_ref, in_ref, out_ref):
    span = source_ref.shape[1]
    wanted = lax.broadcasted_iota(jnp.int32, (span, span), 0) == source_ref[...]
    pick = jnp.where(wanted, 1.0, 0.0).astype(jnp.bfloat16)
    for i in range(NY):
        cols = slice(i * span, (i + 1) * span)
        out_ref[:, cols] = nn(in_ref[:, cols], pick).astype(jnp.bfloat16)


def attention_kernel(q_ref, k_ref, out_ref):
    scale = 1.0 / math.sqrt(HD)
    for head in range(q_ref.shape[1] // HD):
        cols = pl.ds(head * HD, HD)
        scores = nt(q_ref[:, cols], k_ref[:, cols]) * scale
        raised = jnp.exp(scores - jnp.max(scores, axis=-1, keepdims=True))
        out_ref[head] = raised / jnp.sum(raised, axis=-1, keepdims=True)


def tail_kernel(rows_ref, attn_ref, w_ref, wc_ref, own_ref, far_ref, q_any, k_any, v_any, *refs):
    gq_ref, gk_ref, gv_ref, grad_ref, q_ref, k_ref, v_ref, sems = refs
    scale = 1.0 / math.sqrt(HD)
    n_g = NX * NH
    part, depth = q_ref.shape[0] // n_g, w_ref.shape[0] // NY
    copies = [
        pltpu.make_async_copy(src, dst, sems.at[i])
        for i, (src, dst) in enumerate(((v_any, v_ref), (k_any, k_ref), (q_any, q_ref)))
    ]
    for copy in copies:
        copy.start()
    weights = [ref[i * depth:(i + 1) * depth] for i in range(NY) for ref in (w_ref, wc_ref)]
    total = None
    for i in range(NY * NC):
        band = pl.ds(i * depth, depth)
        term = nn(jnp.concatenate([own_ref[:, band], far_ref[:, band]], axis=0), weights[i])
        total = term if total is None else total + term
    for copy in copies:
        copy.wait()
    total = total.astype(jnp.bfloat16)
    for slot in range(n_g):
        row = pl.multiple_of(rows_ref[slot] * part, part)
        grad_ref[pl.ds(row, part), :] = total[slot * part:(slot + 1) * part]
    for head in range(q_ref.shape[1] // HD):
        cols = pl.ds(head * HD, HD)
        grad = grad_ref[:, cols]
        attn = attn_ref[head]
        gv_ref[:, cols] = tn(attn.astype(jnp.bfloat16), grad).astype(jnp.bfloat16)
        probs = nt(grad, v_ref[:, cols])
        inner = jnp.sum(attn * probs, axis=-1, keepdims=True)
        ds = (attn * (probs - inner) * scale).astype(jnp.bfloat16)
        gq_ref[:, cols] = nn(ds, k_ref[:, cols]).astype(jnp.bfloat16)
        gk_ref[:, cols] = tn(ds, q_ref[:, cols]).astype(jnp.bfloat16)


VMEM = pl.BlockSpec(memory_space=pltpu.VMEM)
ANY = pl.BlockSpec(memory_space=pl.ANY)
TAIL_VMEM = 52 * 1024 * 1024
SMEM = pl.BlockSpec(memory_space=pltpu.SMEM)
PARAMS = pltpu.CompilerParams(vmem_limit_bytes=16 * 1024 * 1024)


def shards(queries, attn_keys, attn_values, out_weight, grad_out):
    patches, width = queries.shape[1], queries.shape[2]
    heads = width // HD
    q, k, v = (a.reshape(patches, width) for a in (queries, attn_keys, attn_values))
    part, model = grad_out.shape[1], grad_out.shape[2]
    dp, mp = lax.axis_index("dp"), lax.axis_index("mp")
    core, z = dp % NC, (dp // NC) % NZ

    block = out_weight.shape[0]
    span = NZ * NC * block
    place = np.arange(span)
    slot = (place // block) % NZ
    quad = jnp.asarray((slot & 1) << 3 | (slot & 2) << 1)
    source = (((quad ^ (z & 12)) | jnp.asarray(slot >> 2)) * NC + (jnp.asarray(place // (NZ * block)) ^ core)) * block
    source = source + jnp.asarray(place % block)
    own = pl.pallas_call(
        reorder_kernel,
        out_shape=jax.ShapeDtypeStruct((part, model), jnp.bfloat16),
        in_specs=[VMEM, VMEM],
        out_specs=VMEM,
        compiler_params=PARAMS,
        cost_estimate=pl.CostEstimate(flops=2 * part * model * span, bytes_accessed=4 * part * model, transcendentals=0),
    )(source.astype(jnp.int32).reshape(1, span), grad_out.reshape(part, model))

    weight = out_weight
    arrived = swap(weight, z=8)
    half_way = quarter_turn(own)
    own, arrived = after(own, arrived)
    weight = jnp.concatenate([weight, arrived], 0)
    weight = jnp.concatenate([weight, swap(weight, z=4)], 0)
    own = gather_x(own)
    attn = pl.pallas_call(
        attention_kernel,
        out_shape=jax.ShapeDtypeStruct((heads, patches, patches), jnp.float32),
        in_specs=[VMEM] * 2,
        out_specs=VMEM,
        compiler_params=PARAMS,
        cost_estimate=pl.CostEstimate(flops=2 * patches * patches * width, bytes_accessed=1 << 20, transcendentals=0),
    )(q, k)
    weight, half_way, own = after(weight, half_way, own)
    far = quarter_turn(half_way)
    weight = share_quads(weight)
    far = gather_x(far)
    weight, far, attn = after(weight, far, attn)
    weights = [weight, swap(weight, core=1)]
    half = mp % NH
    rows = jnp.stack([i * NH + h for h in (half, 1 - half) for i in range(NX)]).astype(jnp.int32)

    grad_shape = jax.ShapeDtypeStruct((patches, width), jnp.bfloat16)
    outs = pl.pallas_call(
        tail_kernel,
        out_shape=(grad_shape,) * 3,
        in_specs=[SMEM] + [VMEM] * 5 + [ANY] * 3,
        out_specs=(VMEM,) * 3,
        scratch_shapes=[
            pltpu.VMEM((patches, width), jnp.bfloat16),
            *[pltpu.VMEM((patches, width), jnp.bfloat16)] * 3,
            pltpu.SemaphoreType.DMA((3,)),
        ],
        compiler_params=pltpu.CompilerParams(vmem_limit_bytes=TAIL_VMEM),
        cost_estimate=pl.CostEstimate(flops=2 * patches * width * (model + 4 * patches), bytes_accessed=6 << 20, transcendentals=0),
    )(rows, attn, *weights, own, far, q, k, v)
    return tuple(o.reshape(1, patches, width) for o in outs)


def solution(mesh):
    in_specs = (
        P("dp", None, "mp"),
        P("dp", None, "mp"),
        P("dp", None, "mp"),
        P("dp", "mp"),
        P("dp", "mp", None),
    )
    out_specs = (P("dp", None, "mp"), P("dp", None, "mp"), P("dp", None, "mp"))
    return jax.shard_map(shards, mesh=mesh, in_specs=in_specs, out_specs=out_specs, check_vma=False)
```

```python
import math

import jax
import jax.numpy as jnp
import numpy as np
from jax import lax
from jax.experimental import pallas as pl
from jax.experimental.pallas import tpu as pltpu
from jax.sharding import PartitionSpec as P

HD = 128
AXES = ("dp", "mp")
NY, NZ, NC, NX, NH = 4, 16, 2, 4, 2
Y_ORDER = (0, 2, 1, 3)


def exchange(y=0, z=0, core=0, x=0, half=0):
    pairs = []
    for dp in range(NY * NZ * NC):
        other = dp ^ (y * NZ * NC + z * NC + core)
        for mp in range(NX * NH):
            pairs.append((dp * NX * NH + mp, other * NX * NH + (mp ^ (x * NH + half))))
    return pairs


def swap(value, **moves):
    return lax.ppermute(value, AXES, exchange(**moves))


def gather_x(value):
    groups = [[i * NH + h for i in range(NX)] for h in range(NH)]
    return lax.all_gather(value, "mp", axis_index_groups=groups, axis=0, tiled=True)


def share_quad(value):
    groups = [
        [((y * NZ) + quad * 4 + i) * NC + core for i in range(4)]
        for y in range(NY) for quad in range(NZ // 4) for core in range(NC)
    ]
    copies = jnp.broadcast_to(value[None], (4,) + value.shape)
    shared = lax.all_to_all(copies, "dp", 0, 0, axis_index_groups=groups)
    return shared.reshape(4 * value.shape[0], value.shape[1])


def after(*values):
    return lax.optimization_barrier(values)


def quarter_turn(value):
    pairs = []
    for dp in range(NY * NZ * NC):
        y, z, core = dp // (NZ * NC), dp // NC % NZ, dp % NC
        for mp in range(NX * NH):
            x, half = mp // NH, mp % NH
            ring = (half * NZ + z + (1 - 2 * core) * (NZ // 2)) % (NH * NZ)
            target = (y * NZ + ring % NZ) * NC + core
            pairs.append((dp * NX * NH + mp, target * NX * NH + x * NH + ring // NZ))
    return lax.ppermute(value, AXES, pairs)


def nt(a, b):
    return lax.dot_general(a, b, (((1,), (1,)), ((), ())), preferred_element_type=jnp.float32)


def tn(a, b):
    return lax.dot_general(a, b, (((0,), (0,)), ((), ())), preferred_element_type=jnp.float32)


def nn(a, b):
    return lax.dot_general(a, b, (((1,), (0,)), ((), ())), preferred_element_type=jnp.float32)


def reorder_kernel(y_ref, source_ref, in_ref, out_ref):
    span = source_ref.shape[1]
    wanted = lax.broadcasted_iota(jnp.int32, (span, span), 0) == source_ref[...]
    pick = jnp.where(wanted, 1.0, 0.0).astype(jnp.bfloat16)
    for slot, i in enumerate(Y_ORDER):
        start = pl.multiple_of((y_ref[0] ^ i) * span, span)
        out_ref[:, slot * span:(slot + 1) * span] = nn(in_ref[:, pl.ds(start, span)], pick).astype(jnp.bfloat16)


def attention_kernel(q_ref, k_ref, out_ref):
    scale = 1.0 / math.sqrt(HD)
    for head in range(q_ref.shape[1] // HD):
        cols = pl.ds(head * HD, HD)
        scores = nt(q_ref[:, cols], k_ref[:, cols]) * scale
        raised = jnp.exp(scores - jnp.max(scores, axis=-1, keepdims=True))
        out_ref[head] = raised / jnp.sum(raised, axis=-1, keepdims=True)


def first_half_kernel(w_ref, own_any, far_any, q_any, k_any, v_any, sum_ref, rest_ref, q_ref, k_ref, v_ref, g_ref, band_sems, sems):
    rows, depth = own_any.shape[0], w_ref.shape[0] // NY
    first, later = [], []
    for i in range(NY):
        mine, other, place = pl.ds(NC * i * depth, depth), pl.ds((NC * i + 1) * depth, depth), pl.ds(i * depth, depth)
        for j, src in enumerate((own_any, far_any)):
            half = pl.ds(j * rows, rows)
            first.append(pltpu.make_async_copy(src.at[:, mine], g_ref.at[half, place], band_sems.at[0, i, j]))
            later.append(pltpu.make_async_copy(src.at[:, other], rest_ref.at[half, place], band_sems.at[1, i, j]))
    for i, (src, dst) in enumerate(((v_any, v_ref), (k_any, k_ref), (q_any, q_ref))):
        later.append(pltpu.make_async_copy(src, dst, sems.at[i]))
    for copy in first + later:
        copy.start()
    total = None
    for i in range(NY):
        for copy in first[2 * i:2 * i + 2]:
            copy.wait()
        term = nn(g_ref[:, i * depth:(i + 1) * depth], w_ref[i * depth:(i + 1) * depth])
        total = term if total is None else total + term
    sum_ref[...] = total
    for copy in later:
        copy.wait()


def tail_kernel(rows_ref, attn_ref, wc_ref, sum_ref, rest_ref, q_ref, k_ref, v_ref, gq_ref, gk_ref, gv_ref, grad_ref):
    scale = 1.0 / math.sqrt(HD)
    n_g = NX * NH
    part = q_ref.shape[0] // n_g
    total = sum_ref[...] + nn(rest_ref[...], wc_ref[...])
    total = total.astype(jnp.bfloat16)
    for slot in range(n_g):
        row = pl.multiple_of(rows_ref[slot] * part, part)
        grad_ref[pl.ds(row, part), :] = total[slot * part:(slot + 1) * part]
    for head in range(q_ref.shape[1] // HD):
        cols = pl.ds(head * HD, HD)
        grad = grad_ref[:, cols]
        attn = attn_ref[head]
        gv_ref[:, cols] = tn(attn.astype(jnp.bfloat16), grad).astype(jnp.bfloat16)
        probs = nt(grad, v_ref[:, cols])
        inner = jnp.sum(attn * probs, axis=-1, keepdims=True)
        ds = (attn * (probs - inner) * scale).astype(jnp.bfloat16)
        gq_ref[:, cols] = nn(ds, k_ref[:, cols]).astype(jnp.bfloat16)
        gk_ref[:, cols] = tn(ds, q_ref[:, cols]).astype(jnp.bfloat16)


VMEM = pl.BlockSpec(memory_space=pltpu.VMEM)
ANY = pl.BlockSpec(memory_space=pl.ANY)
FIRST_VMEM = 51 * 1024 * 1024
SMEM = pl.BlockSpec(memory_space=pltpu.SMEM)
PARAMS = pltpu.CompilerParams(vmem_limit_bytes=16 * 1024 * 1024)


def shards(queries, attn_keys, attn_values, out_weight, grad_out):
    patches, width = queries.shape[1], queries.shape[2]
    heads = width // HD
    q, k, v = (a.reshape(patches, width) for a in (queries, attn_keys, attn_values))
    part, model = grad_out.shape[1], grad_out.shape[2]
    dp, mp = lax.axis_index("dp"), lax.axis_index("mp")
    core, z, y = dp % NC, (dp // NC) % NZ, dp // (NC * NZ)

    block = out_weight.shape[0]
    span = NZ * NC * block
    place = np.arange(span)
    slot = (place // block) % NZ
    quad = jnp.asarray((slot & 1) << 3 | (slot & 2) << 1)
    source = (((quad ^ (z & 12)) | jnp.asarray(slot >> 2)) * NC + (jnp.asarray(place // (NZ * block)) ^ core)) * block
    source = source + jnp.asarray(place % block)
    own = pl.pallas_call(
        reorder_kernel,
        out_shape=jax.ShapeDtypeStruct((part, model), jnp.bfloat16),
        in_specs=[SMEM, VMEM, VMEM],
        out_specs=VMEM,
        compiler_params=PARAMS,
        cost_estimate=pl.CostEstimate(flops=2 * part * model * span, bytes_accessed=4 * part * model, transcendentals=0),
    )(y.reshape(1), source.astype(jnp.int32).reshape(1, span), grad_out.reshape(part, model))

    attn = pl.pallas_call(
        attention_kernel,
        out_shape=jax.ShapeDtypeStruct((heads, patches, patches), jnp.float32),
        in_specs=[VMEM] * 2,
        out_specs=VMEM,
        compiler_params=PARAMS,
        cost_estimate=pl.CostEstimate(flops=2 * patches * patches * width, bytes_accessed=1 << 20, transcendentals=0),
    )(q, k)
    weight = out_weight
    arrived = swap(weight, z=8)
    half_way = quarter_turn(own)
    own, arrived = after(own, arrived)
    weight = jnp.concatenate([weight, arrived], 0)
    weight = jnp.concatenate([weight, swap(weight, z=4)], 0)
    own = gather_x(own)
    weight, half_way, own = after(weight, half_way, own)
    far = quarter_turn(half_way)
    weight = share_quad(weight)
    weight = jnp.concatenate([weight] + [swap(weight, y=i) for i in Y_ORDER[1:]], 0)
    far = gather_x(far)
    weight, far, attn = after(weight, far, attn)
    across = swap(weight, core=1)
    half = mp % NH
    rows = jnp.stack([i * NH + h for h in (half, 1 - half) for i in range(NX)]).astype(jnp.int32)

    grad_shape = jax.ShapeDtypeStruct((patches, width), jnp.bfloat16)
    half_width = model // NC
    partial, rest, q_in, k_in, v_in = pl.pallas_call(
        first_half_kernel,
        out_shape=(
            jax.ShapeDtypeStruct((patches, width), jnp.float32),
            jax.ShapeDtypeStruct((patches, half_width), jnp.bfloat16),
            *(grad_shape,) * 3,
        ),
        in_specs=[VMEM] + [ANY] * 5,
        out_specs=(VMEM,) * 5,
        scratch_shapes=[
            pltpu.VMEM((patches, half_width), jnp.bfloat16),
            pltpu.SemaphoreType.DMA((NC, NY, 2)),
            pltpu.SemaphoreType.DMA((3,)),
        ],
        compiler_params=pltpu.CompilerParams(vmem_limit_bytes=FIRST_VMEM),
        cost_estimate=pl.CostEstimate(flops=2 * patches * width * half_width, bytes_accessed=3 << 20, transcendentals=0),
    )(weight, own, far, q, k, v)
    outs = pl.pallas_call(
        tail_kernel,
        out_shape=(grad_shape,) * 3,
        in_specs=[SMEM] + [VMEM] * 7,
        out_specs=(VMEM,) * 3,
        scratch_shapes=[pltpu.VMEM((patches, width), jnp.bfloat16)],
        compiler_params=PARAMS,
        cost_estimate=pl.CostEstimate(flops=2 * patches * width * (half_width + 4 * patches), bytes_accessed=6 << 20, transcendentals=0),
    )(rows, attn, across, partial, rest, q_in, k_in, v_in)
    return tuple(o.reshape(1, patches, width) for o in outs)


def solution(mesh):
    in_specs = (
        P("dp", None, "mp"),
        P("dp", None, "mp"),
        P("dp", None, "mp"),
        P("dp", "mp"),
        P("dp", "mp", None),
    )
    out_specs = (P("dp", None, "mp"), P("dp", None, "mp"), P("dp", None, "mp"))
    return jax.shard_map(shards, mesh=mesh, in_specs=in_specs, out_specs=out_specs, check_vma=False)
```

```python
import math

import jax
import jax.numpy as jnp
import numpy as np
from jax import lax
from jax.experimental import pallas as pl
from jax.experimental.pallas import tpu as pltpu
from jax.sharding import PartitionSpec as P

HD = 128
AXES = ("dp", "mp")
NY, NZ, NC, NX, NH = 4, 16, 2, 4, 2
Y_ORDER = (0, 2, 1, 3)


def exchange(y=0, z=0, core=0, x=0, half=0):
    pairs = []
    for dp in range(NY * NZ * NC):
        other = dp ^ (y * NZ * NC + z * NC + core)
        for mp in range(NX * NH):
            pairs.append((dp * NX * NH + mp, other * NX * NH + (mp ^ (x * NH + half))))
    return pairs


def swap(value, **moves):
    return lax.ppermute(value, AXES, exchange(**moves))


def gather_x(value):
    groups = [[i * NH + h for i in range(NX)] for h in range(NH)]
    return lax.all_gather(value, "mp", axis_index_groups=groups, axis=0, tiled=True)


def share_quad(value):
    groups = [
        [((y * NZ) + quad * 4 + i) * NC + core for i in range(4)]
        for y in range(NY) for quad in range(NZ // 4) for core in range(NC)
    ]
    copies = jnp.broadcast_to(value[None], (4,) + value.shape)
    shared = lax.all_to_all(copies, "dp", 0, 0, axis_index_groups=groups)
    return shared.reshape(4 * value.shape[0], value.shape[1])


def after(*values):
    return lax.optimization_barrier(values)


def quarter_turn(value):
    pairs = []
    for dp in range(NY * NZ * NC):
        y, z, core = dp // (NZ * NC), dp // NC % NZ, dp % NC
        for mp in range(NX * NH):
            x, half = mp // NH, mp % NH
            ring = (half * NZ + z + (1 - 2 * core) * (NZ // 2)) % (NH * NZ)
            target = (y * NZ + ring % NZ) * NC + core
            pairs.append((dp * NX * NH + mp, target * NX * NH + x * NH + ring // NZ))
    return lax.ppermute(value, AXES, pairs)


def nt(a, b):
    return lax.dot_general(a, b, (((1,), (1,)), ((), ())), preferred_element_type=jnp.float32)


def tn(a, b):
    return lax.dot_general(a, b, (((0,), (0,)), ((), ())), preferred_element_type=jnp.float32)


def nn(a, b):
    return lax.dot_general(a, b, (((1,), (0,)), ((), ())), preferred_element_type=jnp.float32)


def reorder_kernel(y_ref, source_ref, in_ref, out_ref):
    span = source_ref.shape[1]
    wanted = lax.broadcasted_iota(jnp.int32, (span, span), 0) == source_ref[...]
    pick = jnp.where(wanted, 1.0, 0.0).astype(jnp.bfloat16)
    for slot, i in enumerate(Y_ORDER):
        start = pl.multiple_of((y_ref[0] ^ i) * span, span)
        out_ref[:, slot * span:(slot + 1) * span] = nn(in_ref[:, pl.ds(start, span)], pick).astype(jnp.bfloat16)


def attention_kernel(q_ref, k_ref, out_ref):
    scale = 1.0 / math.sqrt(HD)
    for head in range(q_ref.shape[1] // HD):
        cols = pl.ds(head * HD, HD)
        scores = nt(q_ref[:, cols], k_ref[:, cols]) * scale
        raised = jnp.exp(scores - jnp.max(scores, axis=-1, keepdims=True))
        out_ref[head] = raised / jnp.sum(raised, axis=-1, keepdims=True)


def first_half_kernel(w_ref, own_any, far_any, q_any, k_any, v_any, sum_ref, rest_ref, q_ref, k_ref, v_ref, g_ref, band_sems, sems):
    rows, depth = own_any.shape[0], w_ref.shape[0] // NY
    first, later = [], []
    for i in range(NY):
        mine, other, place = pl.ds(NC * i * depth, depth), pl.ds((NC * i + 1) * depth, depth), pl.ds(i * depth, depth)
        for j, src in enumerate((own_any, far_any)):
            half = pl.ds(j * rows, rows)
            first.append(pltpu.make_async_copy(src.at[:, mine], g_ref.at[half, place], band_sems.at[0, i, j]))
            later.append(pltpu.make_async_copy(src.at[:, other], rest_ref.at[half, place], band_sems.at[1, i, j]))
    for i, (src, dst) in enumerate(((v_any, v_ref), (k_any, k_ref), (q_any, q_ref))):
        later.append(pltpu.make_async_copy(src, dst, sems.at[i]))
    for copy in first + later:
        copy.start()
    total = None
    for i in range(NY):
        for copy in first[2 * i:2 * i + 2]:
            copy.wait()
        term = nn(g_ref[:, i * depth:(i + 1) * depth], w_ref[i * depth:(i + 1) * depth])
        total = term if total is None else total + term
    sum_ref[...] = total
    for copy in later:
        copy.wait()


def tail_kernel(rows_ref, attn_ref, wc_ref, sum_ref, rest_ref, q_ref, k_ref, v_ref, gq_ref, gk_ref, gv_ref, grad_ref):
    scale = 1.0 / math.sqrt(HD)
    n_g = NX * NH
    part = q_ref.shape[0] // n_g
    total = sum_ref[...] + nn(rest_ref[...], wc_ref[...])
    total = total.astype(jnp.bfloat16)
    for slot in range(n_g):
        row = pl.multiple_of(rows_ref[slot] * part, part)
        grad_ref[pl.ds(row, part), :] = total[slot * part:(slot + 1) * part]
    for head in range(q_ref.shape[1] // HD):
        cols = pl.ds(head * HD, HD)
        grad = grad_ref[:, cols]
        attn = attn_ref[head]
        gv_ref[:, cols] = tn(attn.astype(jnp.bfloat16), grad).astype(jnp.bfloat16)
        probs = nt(grad, v_ref[:, cols])
        inner = jnp.sum(attn * probs, axis=-1, keepdims=True)
        ds = (attn * (probs - inner) * scale).astype(jnp.bfloat16)
        gq_ref[:, cols] = nn(ds, k_ref[:, cols]).astype(jnp.bfloat16)
        gk_ref[:, cols] = tn(ds, q_ref[:, cols]).astype(jnp.bfloat16)


VMEM = pl.BlockSpec(memory_space=pltpu.VMEM)
ANY = pl.BlockSpec(memory_space=pl.ANY)
FIRST_VMEM = 51 * 1024 * 1024
SMEM = pl.BlockSpec(memory_space=pltpu.SMEM)
PARAMS = pltpu.CompilerParams(vmem_limit_bytes=16 * 1024 * 1024)


def shards(queries, attn_keys, attn_values, out_weight, grad_out):
    patches, width = queries.shape[1], queries.shape[2]
    heads = width // HD
    q, k, v = (a.reshape(patches, width) for a in (queries, attn_keys, attn_values))
    part, model = grad_out.shape[1], grad_out.shape[2]
    dp, mp = lax.axis_index("dp"), lax.axis_index("mp")
    core, z, y = dp % NC, (dp // NC) % NZ, dp // (NC * NZ)

    block = out_weight.shape[0]
    span = NZ * NC * block
    place = np.arange(span)
    slot = (place // block) % NZ
    quad = jnp.asarray((slot & 1) << 3 | (slot & 2) << 1)
    def order(z):
        source = ((quad ^ (z & 12)) | jnp.asarray(slot >> 2)) * NC + (jnp.asarray(place // (NZ * block)) ^ core)
        source = source * block + jnp.asarray(place % block)
        return y.reshape(1), source.astype(jnp.int32).reshape(1, span)

    reorder = pl.pallas_call(
        reorder_kernel,
        out_shape=jax.ShapeDtypeStruct((part, model), jnp.bfloat16),
        in_specs=[SMEM, VMEM, VMEM],
        out_specs=VMEM,
        compiler_params=PARAMS,
        cost_estimate=pl.CostEstimate(flops=2 * part * model * span, bytes_accessed=4 * part * model, transcendentals=0),
    )
    own = grad_out.reshape(part, model)

    attn = pl.pallas_call(
        attention_kernel,
        out_shape=jax.ShapeDtypeStruct((heads, patches, patches), jnp.float32),
        in_specs=[VMEM] * 2,
        out_specs=VMEM,
        compiler_params=PARAMS,
        cost_estimate=pl.CostEstimate(flops=2 * patches * patches * width, bytes_accessed=1 << 20, transcendentals=0),
    )(q, k)
    weight = out_weight
    arrived = swap(weight, z=8)
    half_way = quarter_turn(own)
    own, arrived = after(own, arrived)
    own = reorder(*order(z), own)
    weight = jnp.concatenate([weight, arrived], 0)
    weight = jnp.concatenate([weight, swap(weight, z=4)], 0)
    own = gather_x(own)
    weight, half_way, own = after(weight, half_way, own)
    far = quarter_turn(reorder(*order(z ^ (NZ // 2)), half_way))
    weight = share_quad(weight)
    weight = jnp.concatenate([weight] + [swap(weight, y=i) for i in Y_ORDER[1:]], 0)
    far = gather_x(far)
    weight, far, attn = after(weight, far, attn)
    across = swap(weight, core=1)
    half = mp % NH
    rows = jnp.stack([i * NH + h for h in (half, 1 - half) for i in range(NX)]).astype(jnp.int32)

    grad_shape = jax.ShapeDtypeStruct((patches, width), jnp.bfloat16)
    half_width = model // NC
    partial, rest, q_in, k_in, v_in = pl.pallas_call(
        first_half_kernel,
        out_shape=(
            jax.ShapeDtypeStruct((patches, width), jnp.float32),
            jax.ShapeDtypeStruct((patches, half_width), jnp.bfloat16),
            *(grad_shape,) * 3,
        ),
        in_specs=[VMEM] + [ANY] * 5,
        out_specs=(VMEM,) * 5,
        scratch_shapes=[
            pltpu.VMEM((patches, half_width), jnp.bfloat16),
            pltpu.SemaphoreType.DMA((NC, NY, 2)),
            pltpu.SemaphoreType.DMA((3,)),
        ],
        compiler_params=pltpu.CompilerParams(vmem_limit_bytes=FIRST_VMEM),
        cost_estimate=pl.CostEstimate(flops=2 * patches * width * half_width, bytes_accessed=3 << 20, transcendentals=0),
    )(weight, own, far, q, k, v)
    outs = pl.pallas_call(
        tail_kernel,
        out_shape=(grad_shape,) * 3,
        in_specs=[SMEM] + [VMEM] * 7,
        out_specs=(VMEM,) * 3,
        scratch_shapes=[pltpu.VMEM((patches, width), jnp.bfloat16)],
        compiler_params=PARAMS,
        cost_estimate=pl.CostEstimate(flops=2 * patches * width * (half_width + 4 * patches), bytes_accessed=6 << 20, transcendentals=0),
    )(rows, attn, across, partial, rest, q_in, k_in, v_in)
    return tuple(o.reshape(1, patches, width) for o in outs)


def solution(mesh):
    in_specs = (
        P("dp", None, "mp"),
        P("dp", None, "mp"),
        P("dp", None, "mp"),
        P("dp", "mp"),
        P("dp", "mp", None),
    )
    out_specs = (P("dp", None, "mp"), P("dp", None, "mp"), P("dp", None, "mp"))
    return jax.shard_map(shards, mesh=mesh, in_specs=in_specs, out_specs=out_specs, check_vma=False)
```
